256 devices in a mesh: rot: 8 (over x, z_lo), rows: 32 (over z_hi, y, core).
Axes of the slice: x: 4, y: 4, z: 8 (z_hi: 4, z_lo: 2; z = z_hi * 2 + z_lo), core: 2. Of those that a mesh axis runs over, the one named last changes fastest.
Arguments:
- inputs: bfloat16 [512, 256, 128], P('rot', 'rows'), may hold values from -6 to 6
- cotangent: bfloat16 [512, 256, 128], P('rot', 'rows'), may hold values from -6 to 6
- filters: bfloat16 [16, 9, 32, 32], replicated, may hold values from -0.09375 to 0.09375
- bias: float32 [32], replicated, may hold values from -1 to 1
Outputs:
- input_grad: bfloat16 [512, 256, 128], P('rot', 'rows')
- filter_grad: float32 [16, 9, 32, 32], P('rot')
The draws below stay inside these ranges and needn't reach their ends.
All inputs are finite; a program needn't handle non-finite values.
Results may differ from the reference program's by a relative error of at most 0.0049.
Values may be sent and summed in bfloat16 or wider, within the bound.
No kernel may reach another device: no remote copies, remote signals or barrier semaphores. Data moves between devices by JAX's collectives and lax.ppermute only.
A program may use at most 64 MiB of HBM per device.

```python
import jax
import jax.numpy as jnp
from jax import lax

ROT = 16
CH = 32
W = 128
C = 512
H = 256


def steps_of(own_key, extent, cuts, least, high):
    level = 1.0
    for position, blocks in cuts:
        steps = jax.random.uniform(jax.random.fold_in(jax.random.fold_in(own_key, 6), position), (blocks,), jnp.float32, least / len(cuts), high / len(cuts))
        level = level * jnp.repeat(jnp.exp(steps), extent[position] // blocks).reshape((-1,) + (1,) * (len(extent) - 1 - position))
    return level


def normal_values(rng, extent, scale, bound, split=(), kind=jnp.bfloat16):
    loudness = steps_of(rng, extent, split, -0.22, 0.18) if split else 1.0
    entries = jax.random.normal(rng, extent, jnp.float32) * scale * loudness
    return jnp.minimum(jnp.maximum(entries, -bound), bound).astype(kind)


def setup_inputs(seed: int = 0) -> dict:
    arg_keys = jax.random.split(jax.random.key(seed), 5)
    inputs = normal_values(arg_keys[0], (C, H, W), 1.0, 6.0, ((0, 8), (1, 32)))
    cotangent = normal_values(arg_keys[1], (C, H, W), 1.0, 6.0, ((0, 8), (1, 32)))
    filters = normal_values(arg_keys[2], (ROT, 9, CH, CH), (9 * ROT * CH) ** -0.5, 0.09375)
    bias = jnp.clip(jax.random.uniform(arg_keys[3], (CH,), jnp.float32, -1.0, 1.0), -1.0, 1.0)
    return {"inputs": inputs, "cotangent": cotangent, "filters": filters, "bias": bias}


def build_kernel(filters):
    steps = jnp.arange(ROT)
    relative = (steps[None, :] - steps[:, None]) % ROT
    taken = filters[relative]
    taken = jnp.transpose(taken, (0, 3, 1, 4, 2))
    return taken.reshape(ROT * CH, ROT * CH, 3, 3)


def convolve(field, kernel):
    return lax.conv_general_dilated(field[None], kernel, (1, 1), ((1, 1), (1, 1)),
                                    dimension_numbers=("NCHW", "OIHW", "NCHW"),
                                    preferred_element_type=jnp.float32)[0]


def reference(inputs, cotangent, filters, bias):
    kernel = build_kernel(filters)
    channels = ROT * CH
    pre = convolve(inputs, kernel) + jnp.tile(bias, ROT)[:, None, None]
    sigma = jax.nn.sigmoid(pre)
    grad_pre = (cotangent.astype(jnp.float32) * sigma * (1.0 + pre * (1.0 - sigma))).astype(jnp.bfloat16)
    flipped = jnp.transpose(kernel, (1, 0, 2, 3))[:, :, ::-1, ::-1]
    input_grad = convolve(grad_pre, flipped).astype(jnp.bfloat16)
    padded = jnp.pad(inputs, ((0, 0), (1, 1), (1, 1)))
    grad_flat = grad_pre.reshape(channels, -1)
    steps = jnp.arange(ROT)
    out_grid = jnp.broadcast_to(steps[None, :], (ROT, ROT))
    in_grid = (steps[None, :] + steps[:, None]) % ROT
    per_tap = []
    for tap_row in range(3):
        for tap_col in range(3):
            window = padded[:, tap_row:tap_row + H, tap_col:tap_col + W].reshape(channels, -1)
            grad_w = jnp.dot(grad_flat, window.T, preferred_element_type=jnp.float32)
            blocks = grad_w.reshape(ROT, CH, ROT, CH)[out_grid, :, in_grid, :]
            per_tap.append(jnp.sum(blocks, axis=1))
    total = jnp.stack(per_tap, axis=1)
    scale = float(ROT * H * W) ** -0.5
    return input_grad, total * scale
```

```python
import jax
import jax.numpy as jnp
from jax import lax
from jax.experimental import pallas as pl
from jax.experimental.pallas import tpu as pltpu
from jax.sharding import PartitionSpec as P

CH = 32
F32 = jnp.float32
BF16 = jnp.bfloat16


def weight_kernel(fwd_ref, bwd_ref, w_ref, wt_ref):
    for src, dst in ((fwd_ref, w_ref), (bwd_ref, wt_ref)):
        for a in range(3):
            for b in range(3):
                v = src[3 * a + b]
                n = v.shape[1]
                for fine in range(4):
                    t = v
                    if fine:
                        cut = n - CH * fine
                        t = jnp.concatenate([v[:, cut:], v[:, :cut]], axis=1)
                    for coarse in range(n // 128):
                        u = t
                        if coarse:
                            cut = n - 128 * coarse
                            u = jnp.concatenate([t[:, cut:], t[:, :cut]], axis=1)
                        row = b * n + CH * (4 * coarse + fine)
                        dst[row : row + CH, a * n : (a + 1) * n] = u


def shift_right(v):
    lane = lax.broadcasted_iota(jnp.int32, v.shape, 1)
    return jnp.where(lane == 0, 0.0, pltpu.roll(v, 1, 1))


def shift_left(v):
    lane = lax.broadcasted_iota(jnp.int32, v.shape, 1)
    n = v.shape[1]
    return jnp.where(lane == n - 1, 0.0, pltpu.roll(v, n - 1, 1))


def grad_kernel(recv_ref, above_ref, below_ref, w_ref, bias_ref, g_ref, fg_ref, x2_ref):
    groups, two, width = recv_ref.shape
    half = two // 2
    n = groups * half
    rot = n // CH
    x0 = recv_ref[:, :half, :].reshape(n, width)
    cot = recv_ref[:, half:, :].reshape(n, width)
    rows = (above_ref[...], x0, below_ref[...])
    x3 = jnp.concatenate(rows, axis=0)
    for a in range(3):
        x = rows[a]
        turned = jnp.concatenate([x[CH:], x[:CH]], axis=0)
        for rep in range(2):
            x2_ref[a, rep * n : (rep + 1) * n, :width] = x
            x2_ref[a, rep * n : (rep + 1) * n, width:] = turned
    parts = [
        jnp.dot(w_ref[b * n : (b + 1) * n, :], x3, preferred_element_type=F32) for b in range(3)
    ]
    bias = jnp.concatenate([bias_ref[...]] * rot, axis=0)
    pre = parts[1] + shift_right(parts[0]) + shift_left(parts[2]) + bias
    sigma = jax.nn.sigmoid(pre)
    grad = cot.astype(F32) * sigma * (1.0 + pre * (1.0 - sigma))
    own = grad.astype(BF16)
    g_ref[...] = own
    taps = (shift_left(grad).astype(BF16), own, shift_right(grad).astype(BF16))
    blank = jnp.zeros((CH, width), BF16)
    total = [None] * 3
    for p in range(rot // 2):
        sides = []
        for r in (2 * p, 2 * p + 1):
            sides.append(jnp.concatenate([t[CH * r : CH * (r + 1)] for t in taps] + [blank], axis=0))
        g2 = jnp.concatenate(sides, axis=1)
        for a in range(3):
            x = x2_ref[a, 2 * CH * p : 2 * CH * p + n, :]
            d = lax.dot_general(x, g2, (((1,), (1,)), ((), ())), preferred_element_type=F32)
            total[a] = d if total[a] is None else total[a] + d
    for a in range(3):
        fg_ref[:, a] = total[a].reshape(groups, half, 4 * CH)


def input_kernel(above_ref, own_ref, below_ref, wt_ref, out_ref):
    n = own_ref.shape[0]
    g3 = jnp.concatenate([below_ref[...], own_ref[...], above_ref[...]], axis=0)
    parts = [
        jnp.dot(wt_ref[b * n : (b + 1) * n, :], g3, preferred_element_type=F32) for b in range(3)
    ]
    out = parts[1] + shift_left(parts[0]) + shift_right(parts[2])
    out_ref[...] = out.astype(BF16)


LIMIT = pltpu.CompilerParams(vmem_limit_bytes=48 * 1024 * 1024)


def call(kernel, outs, flops, scratch=()):
    return pl.pallas_call(
        kernel,
        out_shape=outs,
        scratch_shapes=list(scratch),
        compiler_params=LIMIT,
        cost_estimate=pl.CostEstimate(flops=flops, bytes_accessed=6_000_000, transcendentals=0),
    )


def shaped(shape, dtype):
    return jax.ShapeDtypeStruct(shape, dtype)


def shards(inputs, cotangent, filters, bias):
    local_ch, band, width = inputs.shape
    rotations, taps = filters.shape[:2]
    n = rotations * CH
    groups = lax.axis_size("rot")
    bands = lax.axis_size("rows")
    total = groups * bands

    with jax.named_scope("to_rows"):
        packed = jnp.concatenate(
            [jnp.transpose(inputs, (1, 0, 2)), jnp.transpose(cotangent, (1, 0, 2))], axis=1
        )
        recv = lax.all_to_all(packed, "rot", 0, 0, tiled=True)
    with jax.named_scope("weights"):
        fwd = jnp.transpose(filters, (1, 2, 0, 3)).reshape(taps, CH, n)
        back = filters[(-jnp.arange(rotations)) % rotations]
        bwd = jnp.transpose(back, (1, 3, 0, 2)).reshape(taps, CH, n)
        w, wt = call(weight_kernel, (shaped((3 * n, 3 * n), BF16),) * 2, 1000)(fwd, bwd)
        bias2 = jnp.broadcast_to(bias[:, None], (CH, width))

    order = ("rot", "rows")

    def place(row):
        return (row % groups) * bands + row // groups

    up = [(place(i), place(i + 1)) for i in range(total - 1)]
    down = [(j, i) for i, j in up]
    with jax.named_scope("input_rows"):
        own = recv[:, :local_ch].reshape(n, width)
        above = lax.ppermute(own, order, up)
        below = lax.ppermute(own, order, down)
    with jax.named_scope("grad"):
        g, part = call(
            grad_kernel,
            (shaped((n, width), BF16), shaped((groups, 3, local_ch, 4 * CH), F32)),
            2 * 18 * n * n * width,
            [pltpu.VMEM((3, 2 * n, 2 * width), BF16)],
        )(recv, above, below, w, bias2)
    with jax.named_scope("filter_rot"):
        got = lax.all_to_all(part.reshape(groups, 3 * local_ch, 4 * CH), "rot", 0, 0, tiled=True)
        mine = jnp.sum(got, axis=0).reshape(3, 2, CH, 4 * CH)
    with jax.named_scope("grad_rows"):
        g_above = lax.ppermute(g, order, up)
        g_below = lax.ppermute(g, order, down)
    with jax.named_scope("input_grad"):
        dx = call(input_kernel, shaped((n, width), BF16), 2 * 9 * n * n * width)(
            g_above, g, g_below, wt
        )
        dx = lax.all_to_all(dx.reshape(groups, local_ch, width), "rot", 0, 0, tiled=True)
        input_grad = jnp.transpose(dx, (1, 0, 2))

    core = lax.axis_index("rows") % 2
    swap = [(i, i ^ 1) for i in range(bands)]

    def turns(step, count):
        perms = []
        for s in range(1, count):
            perms.append([(i, i + ((i // step + s) % count - i // step % count) * step) for i in range(bands)])
        return perms

    def add_four(v, step):
        p1, p2, p3 = [lax.ppermute(v, "rows", perm) for perm in turns(step, 4)]
        return (v + p2) + (p1 + p3)

    with jax.named_scope("filter_core"):
        keep = lax.dynamic_index_in_dim(mine, core, 1, keepdims=False)
        give = lax.dynamic_index_in_dim(mine, 1 - core, 1, keepdims=False)
        v = keep + lax.ppermute(give, "rows", swap)
    with jax.named_scope("filter_y"):
        v = add_four(v, 2)
    with jax.named_scope("filter_z"):
        v = add_four(v, 8)
    with jax.named_scope("filter_out"):
        scale = float(rotations * band * bands * width) ** (-0.5)
        v = v * scale
        other = lax.ppermute(v, "rows", swap)
        both = jnp.where(core == 0, jnp.stack([v, other]), jnp.stack([other, v]))
        both = both[..., : 3 * CH].reshape(2, 3, CH, 3, CH)
        filter_grad = jnp.transpose(both, (0, 1, 3, 4, 2)).reshape(2, taps, CH, CH)
    return input_grad, filter_grad


def solution(mesh):
    return jax.shard_map(
        shards,
        mesh=mesh,
        in_specs=(P("rot", "rows", None), P("rot", "rows", None), P(), P()),
        out_specs=(P("rot", "rows", None), P("rot", None, None, None)),
        check_vma=False,
    )
```

```python
import functools

import jax
import jax.numpy as jnp
from jax import lax
from jax.experimental import pallas as pl
from jax.experimental.pallas import tpu as pltpu
from jax.sharding import PartitionSpec as P

CH = 32
F32 = jnp.float32
BF16 = jnp.bfloat16


def spread(src, dst):
    n = src.shape[2]
    for a in range(3):
        for b in range(3):
            v = src[3 * a + b]
            for fine in range(4):
                t = v
                if fine:
                    cut = n - CH * fine
                    t = jnp.concatenate([v[:, cut:], v[:, :cut]], axis=1)
                for coarse in range(n // 128):
                    u = t
                    if coarse:
                        cut = n - 128 * coarse
                        u = jnp.concatenate([t[:, cut:], t[:, :cut]], axis=1)
                    row = b * n + CH * (4 * coarse + fine)
                    dst[row : row + CH, a * n : (a + 1) * n] = u


def row_of(j, groups):
    return jnp.where(j % 2 == 0, j // 2, groups - 1 - j // 2)


def place_of(k, groups):
    return 2 * k if 2 * k < groups else 2 * (groups - 1 - k) + 1


def turned_rows(v, groups, forth):
    n = v.shape[0]
    local = n // groups
    i = lax.broadcasted_iota(jnp.int32, (n, n), 0)
    j = lax.broadcasted_iota(jnp.int32, (n, n), 1)
    if forth:
        i, j = j, i
    one = (i // groups == j % local) & (i % groups == row_of(j // local, groups))
    return jnp.dot(one.astype(BF16), v, preferred_element_type=F32).astype(BF16)


def pack_kernel(x_ref, c_ref, out_ref):
    groups, two, width = out_ref.shape
    out_ref[:, : two // 2] = turned_rows(x_ref[...], groups, True).reshape(groups, two // 2, width)
    out_ref[:, two // 2 :] = turned_rows(c_ref[...], groups, True).reshape(groups, two // 2, width)


def unpack_kernel(groups, dx_ref, out_ref):
    out_ref[...] = turned_rows(dx_ref[...], groups, False)


def shift_right(v):
    lane = lax.broadcasted_iota(jnp.int32, v.shape, 1)
    return jnp.where(lane == 0, 0.0, pltpu.roll(v, 1, 1))


def shift_left(v):
    lane = lax.broadcasted_iota(jnp.int32, v.shape, 1)
    n = v.shape[1]
    return jnp.where(lane == n - 1, 0.0, pltpu.roll(v, n - 1, 1))


def grad_kernel(recv_ref, above_ref, below_ref, f_ref, bias_ref, g_ref, keep_ref, give_ref, x2_ref, w_ref):
    groups, two, width = recv_ref.shape
    half = two // 2
    n = groups * half
    rot = n // CH
    x0 = recv_ref[:, :half, :].reshape(n, width)
    cot = recv_ref[:, half:, :].reshape(n, width)
    rows = (above_ref[...], x0, below_ref[...])
    x3 = jnp.concatenate(rows, axis=0)
    spread(f_ref, w_ref)
    for a in range(3):
        x = rows[a]
        turned = jnp.concatenate([x[CH:], x[:CH]], axis=0)
        for rep in range(2):
            x2_ref[a, rep * n : (rep + 1) * n, :width] = x
            x2_ref[a, rep * n : (rep + 1) * n, width:] = turned
    parts = [
        jnp.dot(w_ref[b * n : (b + 1) * n, :], x3, preferred_element_type=F32) for b in range(3)
    ]
    bias = jnp.concatenate([bias_ref[...]] * rot, axis=0)
    pre = parts[1] + shift_right(parts[0]) + shift_left(parts[2]) + bias
    sigma = jax.nn.sigmoid(pre)
    grad = cot.astype(F32) * sigma * (1.0 + pre * (1.0 - sigma))
    own = grad.astype(BF16)
    g_ref[...] = own
    taps = (shift_left(grad).astype(BF16), own, shift_right(grad).astype(BF16))
    blank = jnp.zeros((CH, width), BF16)
    total = [None] * 3
    for p in range(rot // 2):
        sides = []
        for r in (2 * p, 2 * p + 1):
            sides.append(jnp.concatenate([t[CH * r : CH * (r + 1)] for t in taps] + [blank], axis=0))
        g2 = jnp.concatenate(sides, axis=1)
        for a in range(3):
            x = x2_ref[a, 2 * CH * p : 2 * CH * p + n, :]
            d = lax.dot_general(x, g2, (((1,), (1,)), ((), ())), preferred_element_type=F32)
            total[a] = d if total[a] is None else total[a] + d
    lane = lax.broadcasted_iota(jnp.int32, (n, 4 * CH), 1)
    first = jnp.where(lane < 3 * CH, total[0], pltpu.roll(total[2], 3 * CH, 1))
    second = jnp.where(lane < 3 * CH, total[1], pltpu.roll(total[2], 2 * CH, 1))
    first = first.reshape(groups, 2, CH, 4 * CH)
    second = second.reshape(groups, 2, CH, 4 * CH)
    third = total[2].reshape(groups, 2, 4, 8, 4 * CH)
    spots = lax.broadcasted_iota(jnp.int32, (groups, 2, 8, 4 * CH), 3) // CH
    last = jnp.zeros((groups, 2, 8, 4 * CH), F32)
    for j in range(4):
        moved = pltpu.roll(third[:, :, j].reshape(-1, 4 * CH), (2 * CH + CH * j) % (4 * CH), 1)
        last = jnp.where(spots == j, moved.reshape(last.shape), last)
    core = lax.axis_index("rows") % 2
    for c in range(2):

        @pl.when(core == c)
        def _():
            for ref, part in ((keep_ref, c), (give_ref, 1 - c)):
                ref[:, :CH] = first[:, part]
                ref[:, CH : 2 * CH] = second[:, part]
                ref[:, 2 * CH :] = last[:, part]


def out_kernel(scale, own_ref, other_ref, out_ref):
    core = lax.axis_index("rows") % 2
    for c in range(2):

        @pl.when(core == c)
        def _():
            for ref, part in ((own_ref, c), (other_ref, 1 - c)):
                v = ref[...] * scale
                for row in range(2):
                    t = v[CH * row : CH * (row + 1)].T
                    for b in range(3):
                        out_ref[part, 3 * row + b] = t[CH * b : CH * (b + 1)]
                    out_ref[part, 6 + row] = t[3 * CH :]
                e = v[2 * CH :]
                e = jnp.concatenate([e[:, CH * j : CH * (j + 1)] for j in range(4)], axis=0)
                out_ref[part, 8] = e.T


def input_kernel(above_ref, own_ref, below_ref, f_ref, out_ref, wt_ref):
    n = own_ref.shape[0]
    spread(f_ref, wt_ref)
    g3 = jnp.concatenate([below_ref[...], own_ref[...], above_ref[...]], axis=0)
    parts = [
        jnp.dot(wt_ref[b * n : (b + 1) * n, :], g3, preferred_element_type=F32) for b in range(3)
    ]
    out = parts[1] + shift_left(parts[0]) + shift_right(parts[2])
    out_ref[...] = out.astype(BF16)


LIMIT = pltpu.CompilerParams(vmem_limit_bytes=20 * 1024 * 1024)


def call(kernel, outs, flops, scratch=()):
    return pl.pallas_call(
        kernel,
        out_shape=outs,
        scratch_shapes=list(scratch),
        compiler_params=LIMIT,
        cost_estimate=pl.CostEstimate(flops=flops, bytes_accessed=6_000_000, transcendentals=0),
    )


def shaped(shape, dtype):
    return jax.ShapeDtypeStruct(shape, dtype)


def shards(inputs, cotangent, filters, bias):
    local_ch, band, width = inputs.shape
    rotations, taps = filters.shape[:2]
    n = rotations * CH
    groups = lax.axis_size("rot")
    bands = lax.axis_size("rows")
    total = groups * bands

    with jax.named_scope("to_rows"):
        packed = call(pack_kernel, shaped((groups, 2 * local_ch, width), BF16), 4 * n * n * width)(
            inputs.reshape(n, width), cotangent.reshape(n, width)
        )
        recv = lax.all_to_all(packed, "rot", 0, 0, tiled=True)
    with jax.named_scope("weights"):
        fwd = jnp.transpose(filters, (1, 2, 0, 3)).reshape(taps, CH, n)
        back = jnp.concatenate([filters[:1], filters[:0:-1]], axis=0)
        bwd = jnp.transpose(back, (1, 3, 0, 2)).reshape(taps, CH, n)
        bias2 = jnp.broadcast_to(bias[:, None], (CH, width))

    order = ("rot", "rows")

    def place(row):
        return place_of(row % groups, groups) * bands + row // groups

    up = [(place(i), place(i + 1)) for i in range(total - 1)]
    down = [(j, i) for i, j in up]
    with jax.named_scope("input_rows"):
        recv, fwd, bwd, bias2 = lax.optimization_barrier((recv, fwd, bwd, bias2))
        own = recv[:, :local_ch].reshape(n, width)
        above = lax.ppermute(own, order, up)
        below = lax.ppermute(own, order, down)
    with jax.named_scope("grad"):
        square = pltpu.VMEM((3 * n, 3 * n), BF16)
        half = shaped((groups, 9 * 8, 4 * CH), F32)
        g, keep, give = call(
            grad_kernel,
            (shaped((n, width), BF16), half, half),
            2 * 18 * n * n * width,
            [pltpu.VMEM((3, 2 * n, 2 * width), BF16), square],
        )(recv, above, below, fwd, bias2)
    swap = [(i, i ^ 1) for i in range(bands)]
    with jax.named_scope("filter_core"):
        part = keep + lax.ppermute(give, "rows", swap)
    with jax.named_scope("filter_rot"):
        got = lax.all_to_all(part, "rot", 0, 0, tiled=True)
    with jax.named_scope("grad_rows"):
        g_above = lax.ppermute(g, order, up)
        g_below = lax.ppermute(g, order, down)
    with jax.named_scope("input_grad"):
        dx = call(input_kernel, shaped((n, width), BF16), 2 * 9 * n * n * width, [square])(
            g_above, g, g_below, bwd
        )
    with jax.named_scope("filter_rot"):
        got, dx = lax.optimization_barrier((got, dx))
        v = jnp.sum(got, axis=0)
    with jax.named_scope("input_grad"):
        dx = lax.all_to_all(dx.reshape(groups, local_ch, width), "rot", 0, 0, tiled=True)
        input_grad = call(
            functools.partial(unpack_kernel, groups), shaped((n, width), BF16), 2 * n * n * width
        )(dx.reshape(n, width)).reshape(inputs.shape)

    def turn(i, step, s):
        now = i // step % 4
        return i + ((now + s) % 4 - now) * step

    def add_four(v, step):
        p1, p2, p3 = [
            lax.ppermute(v, "rows", [(i, turn(i, step, s)) for i in range(bands)]) for s in (1, 2, 3)
        ]
        return (v + p2) + (p1 + p3)

    with jax.named_scope("filter_y"):
        v = add_four(v, 2)
    with jax.named_scope("filter_z"):
        v = add_four(v, 8)
    with jax.named_scope("filter_out"):
        scale = float(rotations * band * bands * width) ** (-0.5)
        other = lax.ppermute(v, "rows", swap)
        filter_grad = call(
            functools.partial(out_kernel, scale), shaped((2, taps, CH, CH), F32), 1000
        )(v, other)
    return input_grad, filter_grad


def solution(mesh):
    return jax.shard_map(
        shards,
        mesh=mesh,
        in_specs=(P("rot", "rows", None), P("rot", "rows", None), P(), P()),
        out_specs=(P("rot", "rows", None), P("rot", None, None, None)),
        check_vma=False,
    )
```

```python
import functools

import jax
import jax.numpy as jnp
from jax import lax
from jax.experimental import pallas as pl
from jax.experimental.pallas import tpu as pltpu
from jax.sharding import PartitionSpec as P

CH = 32
HALO = 2
F32 = jnp.float32
BF16 = jnp.bfloat16


def lanes(shape):
    return lax.broadcasted_iota(jnp.int32, shape, len(shape) - 1)


def spread(src, dst):
    n = src.shape[2]
    for a in range(3):
        for b in range(3):
            v = src[3 * a + b]
            for fine in range(4):
                t = v
                if fine:
                    cut = n - CH * fine
                    t = jnp.concatenate([v[:, cut:], v[:, :cut]], axis=1)
                for coarse in range(n // 128):
                    u = t
                    if coarse:
                        cut = n - 128 * coarse
                        u = jnp.concatenate([t[:, cut:], t[:, :cut]], axis=1)
                    row = b * n + CH * (4 * coarse + fine)
                    dst[row : row + CH, a * n : (a + 1) * n] = u


def exchanged(v, band, forth):
    n = v.shape[0]
    i = lax.broadcasted_iota(jnp.int32, (n, n), 0)
    j = lax.broadcasted_iota(jnp.int32, (n, n), 1)
    if forth:
        i, j = j, i
    one = (i // band == j % (n // band)) & (i % band == j // (n // band))
    return jnp.dot(one.astype(BF16), v, preferred_element_type=F32).astype(BF16)


def turn_kernel(band, x_hbm, c_hbm, tile_ref, far_ref, near_ref, held, sems):
    width = tile_ref.shape[2]
    half = tile_ref.shape[1] // 2
    copies = [pltpu.make_async_copy(src, held.at[i], sems.at[i]) for i, src in enumerate((x_hbm, c_hbm))]
    for copy in copies:
        copy.start()
    upper = lax.axis_index("rows") % 2 == 1
    for part, copy in enumerate(copies):
        copy.wait()
        t = exchanged(held[part], band, True).reshape(band, half, width)
        spot = slice(part * half, (part + 1) * half)
        tile_ref[:, spot] = t
        first, last = t[:HALO], t[band - HALO :]
        for ref, end in ((far_ref, upper), (near_ref, ~upper)):

            @pl.when(end)
            def _():
                ref[:, spot] = last

            @pl.when(~end)
            def _():
                ref[:, spot] = first


def pack_kernel(cols, tile_ref, far_ref, near_ref, out_ref, edge_ref):
    groups = out_ref.shape[0]
    band, both, width = tile_ref.shape
    pitch = cols + 2 * HALO
    lane = lanes((both, width))
    upper = lax.axis_index("rows") % 2
    for c in range(2):

        @pl.when(upper == c)
        def _():
            edge_ref[:HALO] = (near_ref if c else far_ref)[...]
            edge_ref[HALO:] = (far_ref if c else near_ref)[...]

    for j in range(groups):
        parts = [jnp.zeros((both, width), BF16) for _ in range(2)]
        for r in range(band + 2 * HALO):
            if r < HALO:
                v = edge_ref[r]
            elif r < HALO + band:
                v = tile_ref[r - HALO]
            else:
                v = edge_ref[r - band]
            low = pitch * r + max(HALO - cols * j, 0)
            high = pitch * r + min(pitch, width + HALO - cols * j)
            moved = pltpu.roll(v, (pitch * r - cols * j + HALO) % width, 1)
            for h in range(2):
                if low < width * (h + 1) and high > width * h:
                    ok = (lane >= low - width * h) & (lane < high - width * h)
                    parts[h] = jnp.where(ok, moved, parts[h])
        for h in range(2):
            out_ref[j, :, width * h : width * (h + 1)] = parts[h]


def inside(size, band, cols, ring):
    pitch = cols + 2 * HALO
    lane = lanes((1, size))
    row, col = lane // pitch, lane % pitch
    edge = HALO - ring
    return (row >= edge) & (row < band + 2 * HALO - edge) & (col >= edge) & (col < pitch - edge)


def rows_turned(v, by):
    by = by % v.shape[0]
    return jnp.concatenate([v[by:], v[:by]], axis=0) if by else v


def grad_kernel(band, cols, recv_ref, f_ref, bias_ref, g_ref, keep_ref, give_ref, x2_ref, w_ref):
    groups, both, size = recv_ref.shape
    half = both // 2
    n = groups * half
    rot = n // CH
    pitch = cols + 2 * HALO
    x = recv_ref[:, :half, :].reshape(n, size)
    cot = recv_ref[:, half:, :].reshape(n, size)
    x2_ref[:n] = x
    x2_ref[n:] = x
    spread(f_ref, w_ref)
    x3 = jnp.concatenate([pltpu.roll(x, pitch, 1), x, pltpu.roll(x, size - pitch, 1)], axis=0)
    parts = [
        jnp.dot(w_ref[b * n : (b + 1) * n, :], x3, preferred_element_type=F32) for b in range(3)
    ]
    bias = jnp.concatenate([bias_ref[...]] * rot, axis=0)
    pre = parts[1] + pltpu.roll(parts[0], 1, 1) + pltpu.roll(parts[2], size - 1, 1) + bias
    sigma = jax.nn.sigmoid(pre)
    grad = cot.astype(F32) * sigma * (1.0 + pre * (1.0 - sigma))
    grad = jnp.where(inside(size, band, cols, 1), grad, 0.0)
    g_ref[...] = grad.astype(BF16)
    own = jnp.where(inside(size, band, cols, 0), grad, 0.0).astype(BF16)
    moved = [
        pltpu.roll(own, (pitch * (a - 1) + b - 1) % size, 1) if (a, b) != (1, 1) else own
        for a in range(3)
        for b in range(3)
    ]
    nt = (((1,), (1,)), ((), ()))
    total = None
    for r in range(rot):
        g8 = jnp.concatenate([t[CH * r : CH * (r + 1)] for t in moved[:8]], axis=0)
        d = lax.dot_general(x2_ref[CH * r : CH * r + n, :], g8, nt, preferred_element_type=F32)
        total = d if total is None else total + d
    lined = [None] * 4
    for m in range(rot // 8):
        d = lax.dot_general(
            x, moved[8][8 * CH * m : 8 * CH * (m + 1)], nt, preferred_element_type=F32
        )
        for v in range(2):
            for t in range(4):
                e = rows_turned(d[:, 128 * v : 128 * (v + 1)], CH * (8 * m + 4 * v + t))
                lined[t] = e if lined[t] is None else lined[t] + e
    last = lined[0]
    for t in range(1, 4):
        last = last + pltpu.roll(lined[t], 128 - CH * t, 1)
    split = last.reshape(groups, 2, 4, 8, 128)
    spots = lanes((groups * 2 * 8, 128)) // CH
    last = split[:, :, 0].reshape(-1, 128)
    for j in range(1, 4):
        last = jnp.where(spots == j, pltpu.roll(split[:, :, j].reshape(-1, 128), CH * j, 1), last)
    last = last.reshape(groups, 2, 8, 128)
    one = total[:, :128].reshape(groups, 2, CH, 128)
    two = total[:, 128:].reshape(groups, 2, CH, 128)
    core = lax.axis_index("rows") % 2
    for c in range(2):

        @pl.when(core == c)
        def _():
            for ref, part in ((keep_ref, c), (give_ref, 1 - c)):
                ref[:, :CH] = one[:, part]
                ref[:, CH : 2 * CH] = two[:, part]
                ref[:, 2 * CH :] = last[:, part]


def input_kernel(band, cols, g_ref, f_ref, out_ref, w_ref):
    n, size = g_ref.shape
    pitch = cols + 2 * HALO
    spread(f_ref, w_ref)
    g = g_ref[...]
    g3 = jnp.concatenate([pltpu.roll(g, size - pitch, 1), g, pltpu.roll(g, pitch, 1)], axis=0)
    parts = [
        jnp.dot(w_ref[b * n : (b + 1) * n, :], g3, preferred_element_type=F32) for b in range(3)
    ]
    grad = parts[1] + pltpu.roll(parts[0], size - 1, 1) + pltpu.roll(parts[2], 1, 1)
    grad = grad.astype(BF16)
    width = out_ref.shape[1]
    lane = lanes((n, width))
    out = jnp.zeros((n, width), BF16)
    for r in range(band):
        at = pitch * (r + HALO) + HALO
        for h in range(size // width):
            low, high = max(at, width * h), min(at + cols, width * (h + 1))
            if low < high:
                piece = pltpu.roll(grad[:, width * h : width * (h + 1)], (cols * r - at) % width, 1)
                low, high = low - at + cols * r, high - at + cols * r
                out = jnp.where((lane >= low) & (lane < high), piece, out)
    out_ref[...] = out


def join_kernel(keep_ref, other_ref, dx_ref, out_ref):
    groups, terms, width = keep_ref.shape
    local = dx_ref.shape[1]
    out_ref[:, :local] = dx_ref[...]
    sums = keep_ref[...] + other_ref[...]
    pad = jnp.zeros((groups, out_ref.shape[1] - local - terms, width), F32)
    out_ref[:, local:] = jnp.concatenate([sums, pad], axis=1).astype(BF16)


def unpack_kernel(band, cols, dx_ref, out_ref):
    groups, local, width = dx_ref.shape
    lane = lanes((local, width))
    rows = []
    for r in range(band):
        out = jnp.zeros((local, width), BF16)
        for j in range(groups):
            piece = pltpu.roll(dx_ref[j], (cols * (j - r)) % width, 1)
            out = jnp.where((lane >= cols * j) & (lane < cols * (j + 1)), piece, out)
        rows.append(out)
    out_ref[...] = exchanged(jnp.concatenate(rows, axis=0), band, False)


def out_kernel(scale, own_ref, other_ref, out_ref):
    core = lax.axis_index("rows") % 2
    for c in range(2):

        @pl.when(core == c)
        def _():
            for ref, part in ((own_ref, c), (other_ref, 1 - c)):
                v = ref[...] * scale
                for row in range(2):
                    t = v[CH * row : CH * (row + 1)].T
                    for b in range(4):
                        out_ref[part, 4 * row + b] = t[CH * b : CH * (b + 1)]
                e = v[2 * CH :]
                e = jnp.concatenate([e[:, CH * j : CH * (j + 1)] for j in range(4)], axis=0)
                out_ref[part, 8] = e.T


def shaped(shape, dtype):
    return jax.ShapeDtypeStruct(shape, dtype)


def call(kernel, outs, flops, scratch=(), limit=24, **specs):
    return pl.pallas_call(
        kernel,
        out_shape=outs,
        scratch_shapes=list(scratch),
        **specs,
        compiler_params=pltpu.CompilerParams(vmem_limit_bytes=limit * 1024 * 1024),
        cost_estimate=pl.CostEstimate(flops=flops, bytes_accessed=2_000_000, transcendentals=0),
    )


def shards(inputs, cotangent, filters, bias):
    local, band, width = inputs.shape
    rotations, taps = filters.shape[:2]
    n = rotations * CH
    groups = lax.axis_size("rot")
    bands = lax.axis_size("rows")
    cols = width // groups
    size = 2 * width
    across = [(i, j) for i in range(1, bands - 1, 2) for i, j in ((i, i + 1), (i + 1, i))]
    swap = [(i, i ^ 1) for i in range(bands)]
    square = pltpu.VMEM((3 * n, 3 * n), BF16)

    with jax.named_scope("edge_rows"):
        edge = shaped((HALO, 2 * local, width), BF16)
        tile, far, near = call(
            functools.partial(turn_kernel, band),
            (shaped((band, 2 * local, width), BF16), edge, edge),
            4 * n * n * width,
            [pltpu.VMEM((2, n, width), BF16), pltpu.SemaphoreType.DMA((2,))],
            in_specs=[pl.BlockSpec(memory_space=pltpu.HBM)] * 2,
            limit=60,
        )(inputs.reshape(n, width), cotangent.reshape(n, width))
        far = lax.ppermute(far, "rows", across)
        near = lax.ppermute(near, "rows", swap)
    with jax.named_scope("to_tiles"):
        packed = call(
            functools.partial(pack_kernel, cols),
            shaped((groups, 2 * local, size), BF16),
            1000,
            [pltpu.VMEM((2 * HALO, 2 * local, width), BF16)],
            limit=60,
        )(tile, far, near)
        recv = lax.all_to_all(packed, "rot", 0, 0, tiled=True)
    with jax.named_scope("weights"):
        fwd = jnp.transpose(filters, (1, 2, 0, 3)).reshape(taps, CH, n)
        back = jnp.concatenate([filters[:1], filters[:0:-1]], axis=0)
        bwd = jnp.transpose(back, (1, 3, 0, 2)).reshape(taps, CH, n)
        bias2 = jnp.broadcast_to(bias[:, None], (CH, size))
        recv, fwd, bwd, bias2 = lax.optimization_barrier((recv, fwd, bwd, bias2))
    with jax.named_scope("grad"):
        half = shaped((groups, 9 * 8, 4 * CH), F32)
        g, keep, give = call(
            functools.partial(grad_kernel, band, cols),
            (shaped((n, size), BF16), half, half),
            2 * 18 * n * n * size,
            [pltpu.VMEM((2 * n, size), BF16), square],
        )(recv, fwd, bias2)
    def turn(i, step, s):
        now = i // step % 4
        return i + ((now + s) % 4 - now) * step

    def add_four(v, step):
        p1, p2, p3 = [
            lax.ppermute(v, "rows", [(i, turn(i, step, s)) for i in range(bands)]) for s in (1, 2, 3)
        ]
        return (v + p2) + (p1 + p3)

    with jax.named_scope("filter_core"):
        other = lax.ppermute(give, "rows", swap)
    with jax.named_scope("input_grad"):
        dx = call(
            functools.partial(input_kernel, band, cols),
            shaped((n, width), BF16),
            2 * 9 * n * n * size,
            [square],
        )(g, bwd)
    with jax.named_scope("to_channels"):
        terms = keep.shape[1]
        block = local + -(-terms // 16) * 16
        sent = call(join_kernel, shaped((groups, block, width), BF16), 1000)(
            keep, other, dx.reshape(groups, local, width)
        )
        got = lax.all_to_all(sent, "rot", 0, 0, tiled=True)
    with jax.named_scope("filter_rot"):
        v = jnp.sum(got[:, local : local + terms].astype(F32), axis=0)
    with jax.named_scope("input_grad"):
        input_grad = call(
            functools.partial(unpack_kernel, band, cols), shaped((n, width), BF16), 2 * n * n * width
        )(got[:, :local]).reshape(inputs.shape)
    with jax.named_scope("filter_y"):
        v = add_four(v, 2)
    with jax.named_scope("filter_z"):
        v = add_four(v, 8)
    with jax.named_scope("filter_out"):
        scale = float(rotations * band * bands * width) ** (-0.5)
        other = lax.ppermute(v, "rows", swap)
        filter_grad = call(
            functools.partial(out_kernel, scale), shaped((2, taps, CH, CH), F32), 1000
        )(v, other)
    return input_grad, filter_grad


def solution(mesh):
    return jax.shard_map(
        shards,
        mesh=mesh,
        in_specs=(P("rot", "rows", None), P("rot", "rows", None), P(), P()),
        out_specs=(P("rot", "rows", None), P("rot", None, None, None)),
        check_vma=False,
    )
```

```python
import functools

import jax
import jax.numpy as jnp
from jax import lax
from jax.experimental import pallas as pl
from jax.experimental.pallas import tpu as pltpu
from jax.sharding import PartitionSpec as P

CH = 32
HALO = 2
GROUP = 16
F32 = jnp.float32
BF16 = jnp.bfloat16


def lanes(shape):
    return lax.broadcasted_iota(jnp.int32, shape, len(shape) - 1)


def spread(src, dst):
    n = src.shape[2]
    for a in range(3):
        for b in range(3):
            v = src[3 * a + b]
            for fine in range(4):
                t = v
                if fine:
                    cut = n - CH * fine
                    t = jnp.concatenate([v[:, cut:], v[:, :cut]], axis=1)
                for coarse in range(n // 128):
                    u = t
                    if coarse:
                        cut = n - 128 * coarse
                        u = jnp.concatenate([t[:, cut:], t[:, :cut]], axis=1)
                    row = b * n + CH * (4 * coarse + fine)
                    dst[row : row + CH, a * n : (a + 1) * n] = u


def exchanged(v, band, forth):
    n = v.shape[0]
    i = lax.broadcasted_iota(jnp.int32, (n, n), 0)
    j = lax.broadcasted_iota(jnp.int32, (n, n), 1)
    if forth:
        i, j = j, i
    one = (i // band == j % (n // band)) & (i % band == j // (n // band))
    return jnp.dot(one.astype(BF16), v, preferred_element_type=F32).astype(BF16)


def place_row(parts, v, r, j, cols):
    both, width = v.shape
    pitch = cols + 2 * HALO
    lane = lanes((both, width))
    low = pitch * r + max(HALO - cols * j, 0)
    high = pitch * r + min(pitch, width + HALO - cols * j)
    moved = pltpu.roll(v, (pitch * r - cols * j + HALO) % width, 1)
    for h in range(2):
        if low < width * (h + 1) and high > width * h:
            ok = (lane >= low - width * h) & (lane < high - width * h)
            parts[h] = jnp.where(ok, moved, parts[h])


def ends_kernel(band, x_ref, c_ref, far_ref, near_ref):
    n, width = x_ref.shape
    local = n // band
    upper = (lax.axis_index("rows") % 2) * (band - HALO)
    i = lax.broadcasted_iota(jnp.int32, (2 * HALO * local, n), 0)
    j = lax.broadcasted_iota(jnp.int32, (2 * HALO * local, n), 1)
    spot = i // local
    row = spot % HALO + jnp.where(spot < HALO, upper, band - HALO - upper)
    one = ((i % local == j // band) & (row == j % band)).astype(BF16)
    for part, ref in enumerate((x_ref, c_ref)):
        t = jnp.dot(one, ref[...], preferred_element_type=F32).astype(BF16)
        t = t.reshape(2 * HALO, local, width)
        far_ref[:, part * local : (part + 1) * local] = t[:HALO]
        near_ref[:, part * local : (part + 1) * local] = t[HALO:]


def own_kernel(band, cols, x_ref, c_ref, out_ref):
    groups, both, size = out_ref.shape
    width = size // 2
    turned = [
        exchanged(ref[...], band, True).reshape(band, both // 2, width) for ref in (x_ref, c_ref)
    ]
    rows = [jnp.concatenate([t[r] for t in turned], axis=0) for r in range(band)]
    for j in range(groups):
        parts = [jnp.zeros((both, width), BF16) for _ in range(2)]
        for r in range(band):
            place_row(parts, rows[r], r + HALO, j, cols)
        for h in range(2):
            out_ref[j, :, width * h : width * (h + 1)] = parts[h]


def edge_kernel(band, cols, own_ref, far_ref, near_ref, out_ref, edge_ref):
    groups, both, size = out_ref.shape
    width = size // 2
    upper = lax.axis_index("rows") % 2
    for c in range(2):

        @pl.when(upper == c)
        def _():
            edge_ref[:HALO] = (near_ref if c else far_ref)[...]
            edge_ref[HALO:] = (far_ref if c else near_ref)[...]

    for j in range(groups):
        parts = [own_ref[j, :, width * h : width * (h + 1)] for h in range(2)]
        for r in range(HALO):
            place_row(parts, edge_ref[r], r, j, cols)
            place_row(parts, edge_ref[HALO + r], r + HALO + band, j, cols)
        for h in range(2):
            out_ref[j, :, width * h : width * (h + 1)] = parts[h]


def inside(size, band, cols, ring):
    pitch = cols + 2 * HALO
    lane = lanes((1, size))
    row, col = lane // pitch, lane % pitch
    edge = HALO - ring
    return (row >= edge) & (row < band + 2 * HALO - edge) & (col >= edge) & (col < pitch - edge)


def lanes_turned(v, by):
    return jnp.concatenate([v[:, by:], v[:, :by]], axis=1) if by else v


def grad_kernel(band, cols, recv_ref, f_ref, bias_ref, g_ref, keep_ref, give_ref, xt_ref, w_ref):
    groups, both, size = recv_ref.shape
    half = both // 2
    n = groups * half
    rot = n // CH
    pitch = cols + 2 * HALO
    x = recv_ref[:, :half, :].reshape(n, size)
    cot = recv_ref[:, half:, :].reshape(n, size)
    spread(f_ref, w_ref)
    x3 = jnp.concatenate([pltpu.roll(x, pitch, 1), x, pltpu.roll(x, size - pitch, 1)], axis=0)
    parts = [
        jnp.dot(w_ref[b * n : (b + 1) * n, :], x3, preferred_element_type=F32) for b in range(3)
    ]
    bias = jnp.concatenate([bias_ref[...]] * rot, axis=0)
    pre = parts[1] + pltpu.roll(parts[0], 1, 1) + pltpu.roll(parts[2], size - 1, 1) + bias
    sigma = jax.nn.sigmoid(pre)
    grad = cot.astype(F32) * sigma * (1.0 + pre * (1.0 - sigma))
    grad = jnp.where(inside(size, band, cols, 1), grad, 0.0)
    g_ref[...] = grad.astype(BF16)
    own = jnp.where(inside(size, band, cols, 0), grad, 0.0).astype(BF16)
    moved = [
        pltpu.roll(own, (pitch * (a - 1) + b - 1) % size, 1) if (a, b) != (1, 1) else own
        for a in range(3)
        for b in range(3)
    ]
    turned = x.T
    for fine in range(4):
        v = lanes_turned(turned, CH * fine)
        xt_ref[fine, :, :n] = v
        xt_ref[fine, :, n:] = v
    total = None
    for first in range(0, rot, GROUP):
        turns = range(first, first + GROUP)
        g8 = [jnp.concatenate([t[CH * r : CH * (r + 1)] for t in moved[:8]], axis=0) for r in turns]
        xs = [xt_ref[r % 4, :, 128 * (r // 4) : 128 * (r // 4) + n] for r in turns]
        d = jnp.dot(
            jnp.concatenate(g8, axis=1), jnp.concatenate(xs, axis=0), preferred_element_type=F32
        )
        total = d if total is None else total + d
    d = jnp.dot(moved[8], turned, preferred_element_type=F32)
    last = jnp.zeros((CH, n), F32)
    for fine in range(4):
        lined = None
        for coarse in range(rot // 4):
            r = 4 * coarse + fine
            e = lanes_turned(d[CH * r : CH * (r + 1)], 128 * coarse)
            lined = e if lined is None else lined + e
        last = last + lanes_turned(lined, CH * fine)
    spots = lanes((2 * CH, 128)) // CH
    spots8 = lanes((8, 128)) // CH
    taken = []
    for s in range(rot):
        at = slice(128 * (s // 4), 128 * (s // 4 + 1))
        wide = [total[2 * CH * t : 2 * CH * (t + 1), at] for t in range(4)]
        thin = [last[8 * t : 8 * (t + 1), at] for t in range(4)]
        for pieces, where in ((wide, spots), (thin, spots8)):
            out = None
            for t in range(4):
                by = CH * ((t - s) % 4)
                v = pltpu.roll(pieces[t], by, 1) if by else pieces[t]
                out = v if out is None else jnp.where(where == t, v, out)
            taken.append(out)
    core = lax.axis_index("rows") % 2
    for c in range(2):

        @pl.when(core == c)
        def _():
            for ref, part in ((keep_ref, c), (give_ref, 1 - c)):
                for k in range(groups):
                    ref[k, : 2 * CH] = taken[2 * (2 * k + part)]
                    ref[k, 2 * CH :] = taken[2 * (2 * k + part) + 1]


def input_kernel(band, cols, g_ref, f_ref, out_ref, w_ref):
    n, size = g_ref.shape
    pitch = cols + 2 * HALO
    spread(f_ref, w_ref)
    g = g_ref[...]
    g3 = jnp.concatenate([pltpu.roll(g, size - pitch, 1), g, pltpu.roll(g, pitch, 1)], axis=0)
    parts = [
        jnp.dot(w_ref[b * n : (b + 1) * n, :], g3, preferred_element_type=F32) for b in range(3)
    ]
    grad = parts[1] + pltpu.roll(parts[0], size - 1, 1) + pltpu.roll(parts[2], 1, 1)
    grad = grad.astype(BF16)
    width = out_ref.shape[1]
    lane = lanes((n, width))
    out = jnp.zeros((n, width), BF16)
    for r in range(band):
        at = pitch * (r + HALO) + HALO
        for h in range(size // width):
            low, high = max(at, width * h), min(at + cols, width * (h + 1))
            if low < high:
                piece = pltpu.roll(grad[:, width * h : width * (h + 1)], (cols * r - at) % width, 1)
                low, high = low - at + cols * r, high - at + cols * r
                out = jnp.where((lane >= low) & (lane < high), piece, out)
    out_ref[...] = out


def join_kernel(keep_ref, other_ref, dx_ref, out_ref):
    groups, terms, width = keep_ref.shape
    local = dx_ref.shape[1]
    out_ref[:, :local] = dx_ref[...]
    sums = keep_ref[...] + other_ref[...]
    pad = jnp.zeros((groups, out_ref.shape[1] - local - terms, width), F32)
    out_ref[:, local:] = jnp.concatenate([sums, pad], axis=1).astype(BF16)


def unpack_kernel(band, cols, dx_ref, out_ref):
    groups, local, width = dx_ref.shape
    lane = lanes((local, width))
    rows = []
    for r in range(band):
        out = jnp.zeros((local, width), BF16)
        for j in range(groups):
            piece = pltpu.roll(dx_ref[j], (cols * (j - r)) % width, 1)
            out = jnp.where((lane >= cols * j) & (lane < cols * (j + 1)), piece, out)
        rows.append(out)
    out_ref[...] = exchanged(jnp.concatenate(rows, axis=0), band, False)


def out_kernel(scale, own_ref, other_ref, out_ref):
    core = lax.axis_index("rows") % 2
    for c in range(2):

        @pl.when(core == c)
        def _():
            for ref, part in ((own_ref, c), (other_ref, 1 - c)):
                v = ref[...] * scale
                for tap in range(8):
                    row, at = CH * (tap % 2), CH * (tap // 2)
                    out_ref[part, tap] = v[row : row + CH, at : at + CH]
                for t in range(4):
                    out_ref[part, 8, 8 * t : 8 * (t + 1)] = v[2 * CH :, CH * t : CH * (t + 1)]


def shaped(shape, dtype):
    return jax.ShapeDtypeStruct(shape, dtype)


def call(kernel, outs, flops, scratch=(), limit=24, **specs):
    return pl.pallas_call(
        kernel,
        out_shape=outs,
        scratch_shapes=list(scratch),
        **specs,
        compiler_params=pltpu.CompilerParams(vmem_limit_bytes=limit * 1024 * 1024),
        cost_estimate=pl.CostEstimate(flops=flops, bytes_accessed=2_000_000, transcendentals=0),
    )


def shards(inputs, cotangent, filters, bias):
    local, band, width = inputs.shape
    rotations, taps = filters.shape[:2]
    n = rotations * CH
    groups = lax.axis_size("rot")
    bands = lax.axis_size("rows")
    cols = width // groups
    size = 2 * width
    across = [(i, j) for i in range(1, bands - 1, 2) for i, j in ((i, i + 1), (i + 1, i))]
    swap = [(i, i ^ 1) for i in range(bands)]
    square = pltpu.VMEM((3 * n, 3 * n), BF16)

    with jax.named_scope("edge_rows"):
        x, c = inputs.reshape(n, width), cotangent.reshape(n, width)
        edge = shaped((HALO, 2 * local, width), BF16)
        far, near = call(functools.partial(ends_kernel, band), (edge, edge), 1000)(x, c)
        far = lax.ppermute(far, "rows", across)
        near = lax.ppermute(near, "rows", swap)
    with jax.named_scope("to_tiles"):
        tiles = shaped((groups, 2 * local, size), BF16)
        own = call(functools.partial(own_kernel, band, cols), tiles, 4 * n * n * width)(
            x, c
        )
        packed = call(
            functools.partial(edge_kernel, band, cols),
            tiles,
            1000,
            [pltpu.VMEM((2 * HALO, 2 * local, width), BF16)],
        )(own, far, near)
        recv = lax.all_to_all(packed, "rot", 0, 0, tiled=True)
    with jax.named_scope("weights"):
        fwd = jnp.transpose(filters, (1, 2, 0, 3)).reshape(taps, CH, n)
        back = jnp.concatenate([filters[:1], filters[:0:-1]], axis=0)
        bwd = jnp.transpose(back, (1, 3, 0, 2)).reshape(taps, CH, n)
        bias2 = jnp.broadcast_to(bias[:, None], (CH, size))
        recv, fwd, bwd, bias2 = lax.optimization_barrier((recv, fwd, bwd, bias2))
    with jax.named_scope("grad"):
        half = shaped((groups, 9 * 8, 4 * CH), F32)
        g, keep, give = call(
            functools.partial(grad_kernel, band, cols),
            (shaped((n, size), BF16), half, half),
            2 * 18 * n * n * size,
            [pltpu.VMEM((4, size, 2 * n), BF16), square],
        )(recv, fwd, bias2)
    def turn(i, step, s):
        now = i // step % 4
        return i + ((now + s) % 4 - now) * step

    def add_four(v, step, beside=None):
        far, near, back = [
            lax.ppermute(v, "rows", [(i, turn(i, step, s)) for i in range(bands)]) for s in (2, 1, 3)
        ]
        if beside is not None:
            near, far, back, beside = lax.optimization_barrier((near, far, back, beside))
        return (v + far) + (near + back), beside

    with jax.named_scope("filter_core"):
        other = lax.ppermute(give, "rows", swap)
    with jax.named_scope("input_grad"):
        dx = call(
            functools.partial(input_kernel, band, cols),
            shaped((n, width), BF16),
            2 * 9 * n * n * size,
            [square],
        )(g, bwd)
    with jax.named_scope("to_channels"):
        terms = keep.shape[1]
        block = local + -(-terms // 16) * 16
        sent = call(join_kernel, shaped((groups, block, width), BF16), 1000)(
            keep, other, dx.reshape(groups, local, width)
        )
        got = lax.all_to_all(sent, "rot", 0, 0, tiled=True)
    with jax.named_scope("filter_rot"):
        v = jnp.sum(got[:, local : local + terms].astype(F32), axis=0)
    with jax.named_scope("input_grad"):
        input_grad = call(
            functools.partial(unpack_kernel, band, cols), shaped((n, width), BF16), 2 * n * n * width
        )(got[:, :local]).reshape(inputs.shape)
    with jax.named_scope("filter_y"):
        v, _ = add_four(v, 2)
    with jax.named_scope("filter_z"):
        v, input_grad = add_four(v, 8, input_grad)
    with jax.named_scope("filter_out"):
        scale = float(rotations * band * bands * width) ** (-0.5)
        other = lax.ppermute(v, "rows", swap)
        filter_grad = call(
            functools.partial(out_kernel, scale), shaped((2, taps, CH, CH), F32), 1000
        )(v, other)
    return input_grad, filter_grad


def solution(mesh):
    return jax.shard_map(
        shards,
        mesh=mesh,
        in_specs=(P("rot", "rows", None), P("rot", "rows", None), P(), P()),
        out_specs=(P("rot", "rows", None), P("rot", None, None, None)),
        check_vma=False,
    )
```

```python
import functools

import jax
import jax.numpy as jnp
from jax import lax
from jax.experimental import pallas as pl
from jax.experimental.pallas import tpu as pltpu
from jax.sharding import PartitionSpec as P

CH = 32
HALO = 2
GROUP = 16
F32 = jnp.float32
BF16 = jnp.bfloat16


def lanes(shape):
    return lax.broadcasted_iota(jnp.int32, shape, len(shape) - 1)


def spread(src, dst):
    n = src.shape[2]
    for a in range(3):
        for b in range(3):
            v = src[3 * a + b]
            for fine in range(4):
                t = v
                if fine:
                    cut = n - CH * fine
                    t = jnp.concatenate([v[:, cut:], v[:, :cut]], axis=1)
                for coarse in range(n // 128):
                    u = t
                    if coarse:
                        cut = n - 128 * coarse
                        u = jnp.concatenate([t[:, cut:], t[:, :cut]], axis=1)
                    row = b * n + CH * (4 * coarse + fine)
                    dst[row : row + CH, a * n : (a + 1) * n] = u


def exchanged(v, band, forth):
    n = v.shape[0]
    i = lax.broadcasted_iota(jnp.int32, (n, n), 0)
    j = lax.broadcasted_iota(jnp.int32, (n, n), 1)
    if forth:
        i, j = j, i
    one = (i // band == j % (n // band)) & (i % band == j // (n // band))
    return jnp.dot(one.astype(BF16), v, preferred_element_type=F32).astype(BF16)


def place_row(parts, v, r, j, cols):
    both, width = v.shape
    pitch = cols + 2 * HALO
    lane = lanes((both, width))
    low = pitch * r + max(HALO - cols * j, 0)
    high = pitch * r + min(pitch, width + HALO - cols * j)
    moved = pltpu.roll(v, (pitch * r - cols * j + HALO) % width, 1)
    for h in range(2):
        if low < width * (h + 1) and high > width * h:
            ok = (lane >= low - width * h) & (lane < high - width * h)
            parts[h] = jnp.where(ok, moved, parts[h])


def ends_kernel(band, x_ref, c_ref, far_ref, near_ref):
    n, width = x_ref.shape
    local = n // band
    upper = (lax.axis_index("rows") % 2) * (band - HALO)
    i = lax.broadcasted_iota(jnp.int32, (2 * HALO * local, n), 0)
    j = lax.broadcasted_iota(jnp.int32, (2 * HALO * local, n), 1)
    spot = i // local
    row = spot % HALO + jnp.where(spot < HALO, upper, band - HALO - upper)
    one = ((i % local == j // band) & (row == j % band)).astype(BF16)
    for part, ref in enumerate((x_ref, c_ref)):
        t = jnp.dot(one, ref[...], preferred_element_type=F32).astype(BF16)
        t = t.reshape(2 * HALO, local, width)
        far_ref[:, part * local : (part + 1) * local] = t[:HALO]
        near_ref[:, part * local : (part + 1) * local] = t[HALO:]


def own_kernel(band, cols, x_ref, c_ref, out_ref):
    groups, both, size = out_ref.shape
    width = size // 2
    turned = [
        exchanged(ref[...], band, True).reshape(band, both // 2, width) for ref in (x_ref, c_ref)
    ]
    rows = [jnp.concatenate([t[r] for t in turned], axis=0) for r in range(band)]
    for j in range(groups):
        parts = [jnp.zeros((both, width), BF16) for _ in range(2)]
        for r in range(band):
            place_row(parts, rows[r], r + HALO, j, cols)
        for h in range(2):
            out_ref[j, :, width * h : width * (h + 1)] = parts[h]


def edge_kernel(band, cols, own_ref, far_ref, near_ref, out_ref, edge_ref):
    groups, both, size = out_ref.shape
    width = size // 2
    upper = lax.axis_index("rows") % 2
    for c in range(2):

        @pl.when(upper == c)
        def _():
            edge_ref[:HALO] = (near_ref if c else far_ref)[...]
            edge_ref[HALO:] = (far_ref if c else near_ref)[...]

    for j in range(groups):
        parts = [own_ref[j, :, width * h : width * (h + 1)] for h in range(2)]
        for r in range(HALO):
            place_row(parts, edge_ref[r], r, j, cols)
            place_row(parts, edge_ref[HALO + r], r + HALO + band, j, cols)
        for h in range(2):
            out_ref[j, :, width * h : width * (h + 1)] = parts[h]


def inside(size, band, cols, ring):
    pitch = cols + 2 * HALO
    lane = lanes((1, size))
    row, col = lane // pitch, lane % pitch
    edge = HALO - ring
    return (row >= edge) & (row < band + 2 * HALO - edge) & (col >= edge) & (col < pitch - edge)


def lanes_turned(v, by):
    return jnp.concatenate([v[:, by:], v[:, :by]], axis=1) if by else v


def grad_kernel(band, cols, recv_ref, f_ref, bias_ref, g_ref, keep_ref, give_ref, xt_ref, w_ref):
    groups, both, size = recv_ref.shape
    half = both // 2
    n = groups * half
    rot = n // CH
    pitch = cols + 2 * HALO
    x = recv_ref[:, :half, :].reshape(n, size)
    cot = recv_ref[:, half:, :].reshape(n, size)
    spread(f_ref, w_ref)
    x3 = jnp.concatenate([pltpu.roll(x, pitch, 1), x, pltpu.roll(x, size - pitch, 1)], axis=0)
    parts = [
        jnp.dot(w_ref[b * n : (b + 1) * n, :], x3, preferred_element_type=F32) for b in range(3)
    ]
    bias = jnp.concatenate([bias_ref[...]] * rot, axis=0)
    pre = parts[1] + pltpu.roll(parts[0], 1, 1) + pltpu.roll(parts[2], size - 1, 1) + bias
    sigma = jax.nn.sigmoid(pre)
    grad = cot.astype(F32) * sigma * (1.0 + pre * (1.0 - sigma))
    grad = jnp.where(inside(size, band, cols, 1), grad, 0.0)
    g_ref[...] = grad.astype(BF16)
    own = jnp.where(inside(size, band, cols, 0), grad, 0.0).astype(BF16)
    moved = [
        pltpu.roll(own, (pitch * (a - 1) + b - 1) % size, 1) if (a, b) != (1, 1) else own
        for a in range(3)
        for b in range(3)
    ]
    turned = x.T
    for fine in range(4):
        v = lanes_turned(turned, CH * fine)
        xt_ref[fine, :, :n] = v
        xt_ref[fine, :, n:] = v
    total = None
    for first in range(0, rot, GROUP):
        turns = range(first, first + GROUP)
        g8 = [jnp.concatenate([t[CH * r : CH * (r + 1)] for t in moved[:8]], axis=0) for r in turns]
        xs = [xt_ref[r % 4, :, 128 * (r // 4) : 128 * (r // 4) + n] for r in turns]
        d = jnp.dot(
            jnp.concatenate(g8, axis=1), jnp.concatenate(xs, axis=0), preferred_element_type=F32
        )
        total = d if total is None else total + d
    d = jnp.dot(moved[8], turned, preferred_element_type=F32)
    last = jnp.zeros((CH, n), F32)
    for fine in range(4):
        lined = None
        for coarse in range(rot // 4):
            r = 4 * coarse + fine
            e = lanes_turned(d[CH * r : CH * (r + 1)], 128 * coarse)
            lined = e if lined is None else lined + e
        last = last + lanes_turned(lined, CH * fine)
    spots = lanes((2 * CH, 128)) // CH
    spots8 = lanes((8, 128)) // CH
    taken = []
    for s in range(rot):
        at = slice(128 * (s // 4), 128 * (s // 4 + 1))
        wide = [total[2 * CH * t : 2 * CH * (t + 1), at] for t in range(4)]
        thin = [last[8 * t : 8 * (t + 1), at] for t in range(4)]
        for pieces, where in ((wide, spots), (thin, spots8)):
            out = None
            for t in range(4):
                by = CH * ((t - s) % 4)
                v = pltpu.roll(pieces[t], by, 1) if by else pieces[t]
                out = v if out is None else jnp.where(where == t, v, out)
            taken.append(out)
    core = lax.axis_index("rows") % 2
    for c in range(2):

        @pl.when(core == c)
        def _():
            for ref, part in ((keep_ref, c), (give_ref, 1 - c)):
                for k in range(groups):
                    ref[k, : 2 * CH] = taken[2 * (2 * k + part)]
                    ref[k, 2 * CH :] = taken[2 * (2 * k + part) + 1]


def input_kernel(band, cols, g_ref, f_ref, out_ref, w_ref):
    n, size = g_ref.shape
    pitch = cols + 2 * HALO
    spread(f_ref, w_ref)
    g = g_ref[...]
    g3 = jnp.concatenate([pltpu.roll(g, size - pitch, 1), g, pltpu.roll(g, pitch, 1)], axis=0)
    parts = [
        jnp.dot(w_ref[b * n : (b + 1) * n, :], g3, preferred_element_type=F32) for b in range(3)
    ]
    grad = parts[1] + pltpu.roll(parts[0], size - 1, 1) + pltpu.roll(parts[2], 1, 1)
    grad = grad.astype(BF16)
    width = out_ref.shape[1]
    lane = lanes((n, width))
    out = jnp.zeros((n, width), BF16)
    for r in range(band):
        at = pitch * (r + HALO) + HALO
        for h in range(size // width):
            low, high = max(at, width * h), min(at + cols, width * (h + 1))
            if low < high:
                piece = pltpu.roll(grad[:, width * h : width * (h + 1)], (cols * r - at) % width, 1)
                low, high = low - at + cols * r, high - at + cols * r
                out = jnp.where((lane >= low) & (lane < high), piece, out)
    out_ref[...] = out


def join_kernel(keep_ref, other_ref, dx_ref, out_ref):
    groups, terms, width = keep_ref.shape
    local = dx_ref.shape[1]
    out_ref[:, :local] = dx_ref[...]
    sums = keep_ref[...] + other_ref[...]
    pad = jnp.zeros((groups, out_ref.shape[1] - local - terms, width), F32)
    out_ref[:, local:] = jnp.concatenate([sums, pad], axis=1).astype(BF16)


def unpack_kernel(band, cols, dx_ref, out_ref):
    groups, local, width = dx_ref.shape
    lane = lanes((local, width))
    rows = []
    for r in range(band):
        out = jnp.zeros((local, width), BF16)
        for j in range(groups):
            piece = pltpu.roll(dx_ref[j], (cols * (j - r)) % width, 1)
            out = jnp.where((lane >= cols * j) & (lane < cols * (j + 1)), piece, out)
        rows.append(out)
    out_ref[...] = exchanged(jnp.concatenate(rows, axis=0), band, False)


def out_kernel(scale, own_ref, other_ref, out_ref):
    core = lax.axis_index("rows") % 2
    for c in range(2):

        @pl.when(core == c)
        def _():
            for ref, part in ((own_ref, c), (other_ref, 1 - c)):
                v = ref[...] * scale
                for tap in range(8):
                    row, at = CH * (tap % 2), CH * (tap // 2)
                    out_ref[part, tap] = v[row : row + CH, at : at + CH]
                for t in range(4):
                    out_ref[part, 8, 8 * t : 8 * (t + 1)] = v[2 * CH :, CH * t : CH * (t + 1)]


def shaped(shape, dtype):
    return jax.ShapeDtypeStruct(shape, dtype)


def call(kernel, outs, flops, scratch=(), limit=24, **specs):
    return pl.pallas_call(
        kernel,
        out_shape=outs,
        scratch_shapes=list(scratch),
        **specs,
        compiler_params=pltpu.CompilerParams(vmem_limit_bytes=limit * 1024 * 1024),
        cost_estimate=pl.CostEstimate(flops=flops, bytes_accessed=2_000_000, transcendentals=0),
    )


def shards(inputs, cotangent, filters, bias):
    local, band, width = inputs.shape
    rotations, taps = filters.shape[:2]
    n = rotations * CH
    groups = lax.axis_size("rot")
    bands = lax.axis_size("rows")
    cols = width // groups
    size = 2 * width
    across = [(i, j) for i in range(1, bands - 1, 2) for i, j in ((i, i + 1), (i + 1, i))]
    swap = [(i, i ^ 1) for i in range(bands)]
    square = pltpu.VMEM((3 * n, 3 * n), BF16)

    with jax.named_scope("edge_rows"):
        x, c = inputs.reshape(n, width), cotangent.reshape(n, width)
        edge = shaped((HALO, 2 * local, width), BF16)
        far, near = call(functools.partial(ends_kernel, band), (edge, edge), 1000, limit=60)(x, c)
        far = lax.ppermute(far, "rows", across)
        near = lax.ppermute(near, "rows", swap)
    with jax.named_scope("to_tiles"):
        tiles = shaped((groups, 2 * local, size), BF16)
        own = call(functools.partial(own_kernel, band, cols), tiles, 4 * n * n * width)(
            x, c
        )
        packed = call(
            functools.partial(edge_kernel, band, cols),
            tiles,
            1000,
            [pltpu.VMEM((2 * HALO, 2 * local, width), BF16)],
        )(own, far, near)
        recv = lax.all_to_all(packed, "rot", 0, 0, tiled=True)
    with jax.named_scope("weights"):
        fwd = jnp.transpose(filters, (1, 2, 0, 3)).reshape(taps, CH, n)
        back = jnp.concatenate([filters[:1], filters[:0:-1]], axis=0)
        bwd = jnp.transpose(back, (1, 3, 0, 2)).reshape(taps, CH, n)
        bias2 = jnp.broadcast_to(bias[:, None], (CH, size))
        recv, fwd, bwd, bias2 = lax.optimization_barrier((recv, fwd, bwd, bias2))
    with jax.named_scope("grad"):
        half = shaped((groups, 9 * 8, 4 * CH), F32)
        g, keep, give = call(
            functools.partial(grad_kernel, band, cols),
            (shaped((n, size), BF16), half, half),
            2 * 18 * n * n * size,
            [pltpu.VMEM((4, size, 2 * n), BF16), square],
        )(recv, fwd, bias2)
    def met(i, along, pair):
        now = i // along % 4
        return i + (pair(now) - now) * along

    def add_four(v, pair, beside=None):
        def swapped(to):
            return lax.ppermute(v, "rows", [(i, to(i)) for i in range(bands)])

        both = swapped(lambda i: met(met(i, 2, pair), 8, pair))
        deep = swapped(lambda i: met(i, 8, pair))
        wide = swapped(lambda i: met(i, 2, pair))
        if beside is not None:
            both, deep, wide, beside = lax.optimization_barrier((both, deep, wide, beside))
        return (v + both) + (deep + wide), beside

    with jax.named_scope("filter_core"):
        other = lax.ppermute(give, "rows", swap)
    with jax.named_scope("input_grad"):
        dx = call(
            functools.partial(input_kernel, band, cols),
            shaped((n, width), BF16),
            2 * 9 * n * n * size,
            [square],
        )(g, bwd)
    with jax.named_scope("to_channels"):
        terms = keep.shape[1]
        block = local + -(-terms // 16) * 16
        sent = call(join_kernel, shaped((groups, block, width), BF16), 1000)(
            keep, other, dx.reshape(groups, local, width)
        )
        got = lax.all_to_all(sent, "rot", 0, 0, tiled=True)
    with jax.named_scope("filter_rot"):
        v = jnp.sum(got[:, local : local + terms].astype(F32), axis=0)
    with jax.named_scope("input_grad"):
        input_grad = call(
            functools.partial(unpack_kernel, band, cols), shaped((n, width), BF16), 2 * n * n * width
        )(got[:, :local]).reshape(inputs.shape)
    with jax.named_scope("filter_blocks"):
        v, _ = add_four(v, lambda k: k ^ 1)
    with jax.named_scope("filter_rows"):
        v, input_grad = add_four(v, lambda k: 3 - k, input_grad)
    with jax.named_scope("filter_out"):
        scale = float(rotations * band * bands * width) ** (-0.5)
        other = lax.ppermute(v, "rows", swap)
        filter_grad = call(
            functools.partial(out_kernel, scale), shaped((2, taps, CH, CH), F32), 1000
        )(v, other)
    return input_grad, filter_grad


def solution(mesh):
    return jax.shard_map(
        shards,
        mesh=mesh,
        in_specs=(P("rot", "rows", None), P("rot", "rows", None), P(), P()),
        out_specs=(P("rot", "rows", None), P("rot", None, None, None)),
        check_vma=False,
    )
```

```python
import functools

import jax
import jax.numpy as jnp
from jax import lax
from jax.experimental import pallas as pl
from jax.experimental.pallas import tpu as pltpu
from jax.sharding import PartitionSpec as P

CH = 32
HALO = 2
GROUP = 16
F32 = jnp.float32
BF16 = jnp.bfloat16


def lanes(shape):
    return lax.broadcasted_iota(jnp.int32, shape, len(shape) - 1)


def spread(src, dst):
    n = src.shape[2]
    for a in range(3):
        for b in range(3):
            v = src[3 * a + b]
            for fine in range(4):
                t = v
                if fine:
                    cut = n - CH * fine
                    t = jnp.concatenate([v[:, cut:], v[:, :cut]], axis=1)
                for coarse in range(n // 128):
                    u = t
                    if coarse:
                        cut = n - 128 * coarse
                        u = jnp.concatenate([t[:, cut:], t[:, :cut]], axis=1)
                    row = b * n + CH * (4 * coarse + fine)
                    dst[row : row + CH, a * n : (a + 1) * n] = u


def exchanged(v, band, forth):
    n = v.shape[0]
    i = lax.broadcasted_iota(jnp.int32, (n, n), 0)
    j = lax.broadcasted_iota(jnp.int32, (n, n), 1)
    if forth:
        i, j = j, i
    one = (i // band == j % (n // band)) & (i % band == j // (n // band))
    return jnp.dot(one.astype(BF16), v, preferred_element_type=F32).astype(BF16)


def place_row(parts, v, r, j, cols):
    both, width = v.shape
    pitch = cols + 2 * HALO
    lane = lanes((both, width))
    low = pitch * r + max(HALO - cols * j, 0)
    high = pitch * r + min(pitch, width + HALO - cols * j)
    moved = pltpu.roll(v, (pitch * r - cols * j + HALO) % width, 1)
    for h in range(2):
        if low < width * (h + 1) and high > width * h:
            ok = (lane >= low - width * h) & (lane < high - width * h)
            parts[h] = jnp.where(ok, moved, parts[h])


def ends_kernel(band, x_ref, c_ref, far_ref, near_ref):
    n, width = x_ref.shape
    local = n // band
    upper = (lax.axis_index("rows") % 2) * (band - HALO)
    i = lax.broadcasted_iota(jnp.int32, (2 * HALO * local, n), 0)
    j = lax.broadcasted_iota(jnp.int32, (2 * HALO * local, n), 1)
    spot = i // local
    row = spot % HALO + jnp.where(spot < HALO, upper, band - HALO - upper)
    one = ((i % local == j // band) & (row == j % band)).astype(BF16)
    for part, ref in enumerate((x_ref, c_ref)):
        t = jnp.dot(one, ref[...], preferred_element_type=F32).astype(BF16)
        t = t.reshape(2 * HALO, local, width)
        far_ref[:, part * local : (part + 1) * local] = t[:HALO]
        near_ref[:, part * local : (part + 1) * local] = t[HALO:]


def own_kernel(band, cols, x_ref, c_ref, out_ref):
    groups, both, size = out_ref.shape
    width = size // 2
    turned = [
        exchanged(ref[...], band, True).reshape(band, both // 2, width) for ref in (x_ref, c_ref)
    ]
    rows = [jnp.concatenate([t[r] for t in turned], axis=0) for r in range(band)]
    for j in range(groups):
        parts = [jnp.zeros((both, width), BF16) for _ in range(2)]
        for r in range(band):
            place_row(parts, rows[r], r + HALO, j, cols)
        for h in range(2):
            out_ref[j, :, width * h : width * (h + 1)] = parts[h]


def edge_kernel(band, cols, own_ref, far_ref, near_ref, out_ref, edge_ref):
    groups, both, size = out_ref.shape
    width = size // 2
    upper = lax.axis_index("rows") % 2
    for c in range(2):

        @pl.when(upper == c)
        def _():
            edge_ref[:HALO] = (near_ref if c else far_ref)[...]
            edge_ref[HALO:] = (far_ref if c else near_ref)[...]

    for j in range(groups):
        parts = [own_ref[j, :, width * h : width * (h + 1)] for h in range(2)]
        for r in range(HALO):
            place_row(parts, edge_ref[r], r, j, cols)
            place_row(parts, edge_ref[HALO + r], r + HALO + band, j, cols)
        for h in range(2):
            out_ref[j, :, width * h : width * (h + 1)] = parts[h]


def inside(size, band, cols, ring):
    pitch = cols + 2 * HALO
    lane = lanes((1, size))
    row, col = lane // pitch, lane % pitch
    edge = HALO - ring
    return (row >= edge) & (row < band + 2 * HALO - edge) & (col >= edge) & (col < pitch - edge)


def lanes_turned(v, by):
    return jnp.concatenate([v[:, by:], v[:, :by]], axis=1) if by else v


def grad_kernel(band, cols, recv_ref, f_ref, bias_ref, g_ref, keep_ref, give_ref, xt_ref, w_ref):
    groups, both, size = recv_ref.shape
    half = both // 2
    n = groups * half
    rot = n // CH
    pitch = cols + 2 * HALO
    x = recv_ref[:, :half, :].reshape(n, size)
    cot = recv_ref[:, half:, :].reshape(n, size)
    spread(f_ref, w_ref)
    x3 = jnp.concatenate([pltpu.roll(x, pitch, 1), x, pltpu.roll(x, size - pitch, 1)], axis=0)
    parts = [
        jnp.dot(w_ref[b * n : (b + 1) * n, :], x3, preferred_element_type=F32) for b in range(3)
    ]
    bias = jnp.concatenate([bias_ref[...]] * rot, axis=0)
    pre = parts[1] + pltpu.roll(parts[0], 1, 1) + pltpu.roll(parts[2], size - 1, 1) + bias
    sigma = jax.nn.sigmoid(pre)
    grad = cot.astype(F32) * sigma * (1.0 + pre * (1.0 - sigma))
    grad = jnp.where(inside(size, band, cols, 1), grad, 0.0)
    g_ref[...] = grad.astype(BF16)
    own = jnp.where(inside(size, band, cols, 0), grad, 0.0).astype(BF16)
    moved = [
        pltpu.roll(own, (pitch * (a - 1) + b - 1) % size, 1) if (a, b) != (1, 1) else own
        for a in range(3)
        for b in range(3)
    ]
    turned = x.T
    for fine in range(4):
        v = lanes_turned(turned, CH * fine)
        xt_ref[fine, :, :n] = v
        xt_ref[fine, :, n:] = v
    total = None
    for first in range(0, rot, GROUP):
        turns = range(first, first + GROUP)
        g8 = [jnp.concatenate([t[CH * r : CH * (r + 1)] for t in moved[:8]], axis=0) for r in turns]
        xs = [xt_ref[r % 4, :, 128 * (r // 4) : 128 * (r // 4) + n] for r in turns]
        d = jnp.dot(
            jnp.concatenate(g8, axis=1), jnp.concatenate(xs, axis=0), preferred_element_type=F32
        )
        total = d if total is None else total + d
    d = jnp.dot(moved[8], turned, preferred_element_type=F32)
    last = jnp.zeros((CH, n), F32)
    for fine in range(4):
        lined = None
        for coarse in range(rot // 4):
            r = 4 * coarse + fine
            e = lanes_turned(d[CH * r : CH * (r + 1)], 128 * coarse)
            lined = e if lined is None else lined + e
        last = last + lanes_turned(lined, CH * fine)
    spots = lanes((2 * CH, 128)) // CH
    spots8 = lanes((8, 128)) // CH
    taken = []
    for s in range(rot):
        at = slice(128 * (s // 4), 128 * (s // 4 + 1))
        wide = [total[2 * CH * t : 2 * CH * (t + 1), at] for t in range(4)]
        thin = [last[8 * t : 8 * (t + 1), at] for t in range(4)]
        for pieces, where in ((wide, spots), (thin, spots8)):
            out = None
            for t in range(4):
                by = CH * ((t - s) % 4)
                v = pltpu.roll(pieces[t], by, 1) if by else pieces[t]
                out = v if out is None else jnp.where(where == t, v, out)
            taken.append(out)
    core = lax.axis_index("rows") % 2
    for c in range(2):

        @pl.when(core == c)
        def _():
            for ref, part in ((keep_ref, c), (give_ref, 1 - c)):
                for k in range(groups):
                    ref[k, : 2 * CH] = taken[2 * (2 * k + part)]
                    ref[k, 2 * CH :] = taken[2 * (2 * k + part) + 1]


def input_kernel(band, cols, g_ref, f_ref, out_ref, w_ref):
    n, size = g_ref.shape
    pitch = cols + 2 * HALO
    spread(f_ref, w_ref)
    g = g_ref[...]
    g3 = jnp.concatenate([pltpu.roll(g, size - pitch, 1), g, pltpu.roll(g, pitch, 1)], axis=0)
    parts = [
        jnp.dot(w_ref[b * n : (b + 1) * n, :], g3, preferred_element_type=F32) for b in range(3)
    ]
    grad = parts[1] + pltpu.roll(parts[0], size - 1, 1) + pltpu.roll(parts[2], 1, 1)
    grad = grad.astype(BF16)
    width = out_ref.shape[1]
    lane = lanes((n, width))
    out = jnp.zeros((n, width), BF16)
    for r in range(band):
        at = pitch * (r + HALO) + HALO
        for h in range(size // width):
            low, high = max(at, width * h), min(at + cols, width * (h + 1))
            if low < high:
                piece = pltpu.roll(grad[:, width * h : width * (h + 1)], (cols * r - at) % width, 1)
                low, high = low - at + cols * r, high - at + cols * r
                out = jnp.where((lane >= low) & (lane < high), piece, out)
    out_ref[...] = out


def join_kernel(keep_ref, other_ref, dx_ref, out_ref):
    groups, terms, width = keep_ref.shape
    local = dx_ref.shape[1]
    out_ref[:, :local] = dx_ref[...]
    sums = keep_ref[...] + other_ref[...]
    pad = jnp.zeros((groups, out_ref.shape[1] - local - terms, width), F32)
    out_ref[:, local:] = jnp.concatenate([sums, pad], axis=1).astype(BF16)


def unpack_kernel(band, cols, dx_ref, out_ref):
    groups, local, width = dx_ref.shape
    lane = lanes((local, width))
    rows = []
    for r in range(band):
        out = jnp.zeros((local, width), BF16)
        for j in range(groups):
            piece = pltpu.roll(dx_ref[j], (cols * (j - r)) % width, 1)
            out = jnp.where((lane >= cols * j) & (lane < cols * (j + 1)), piece, out)
        rows.append(out)
    out_ref[...] = exchanged(jnp.concatenate(rows, axis=0), band, False)


def out_kernel(scale, own_ref, other_ref, out_ref):
    core = lax.axis_index("rows") % 2
    for c in range(2):

        @pl.when(core == c)
        def _():
            for ref, part in ((own_ref, c), (other_ref, 1 - c)):
                v = ref[...] * scale
                for tap in range(8):
                    row, at = CH * (tap % 2), CH * (tap // 2)
                    out_ref[part, tap] = v[row : row + CH, at : at + CH]
                for t in range(4):
                    out_ref[part, 8, 8 * t : 8 * (t + 1)] = v[2 * CH :, CH * t : CH * (t + 1)]


def shaped(shape, dtype):
    return jax.ShapeDtypeStruct(shape, dtype)


def call(kernel, outs, flops, scratch=(), limit=24, **specs):
    return pl.pallas_call(
        kernel,
        out_shape=outs,
        scratch_shapes=list(scratch),
        **specs,
        compiler_params=pltpu.CompilerParams(vmem_limit_bytes=limit * 1024 * 1024),
        cost_estimate=pl.CostEstimate(flops=flops, bytes_accessed=2_000_000, transcendentals=0),
    )


def shards(inputs, cotangent, filters, bias):
    local, band, width = inputs.shape
    rotations, taps = filters.shape[:2]
    n = rotations * CH
    groups = lax.axis_size("rot")
    bands = lax.axis_size("rows")
    cols = width // groups
    size = 2 * width
    across = [(i, j) for i in range(1, bands - 1, 2) for i, j in ((i, i + 1), (i + 1, i))]
    swap = [(i, i ^ 1) for i in range(bands)]
    square = pltpu.VMEM((3 * n, 3 * n), BF16)

    with jax.named_scope("edge_rows"):
        x, c = inputs.reshape(n, width), cotangent.reshape(n, width)
        edge = shaped((HALO, 2 * local, width), BF16)
        far, near = call(functools.partial(ends_kernel, band), (edge, edge), 1000)(x, c)
        far = lax.ppermute(far, "rows", across)
        near = lax.ppermute(near, "rows", swap)
    with jax.named_scope("to_tiles"):
        tiles = shaped((groups, 2 * local, size), BF16)
        own = call(functools.partial(own_kernel, band, cols), tiles, 4 * n * n * width)(
            x, c
        )
        packed = call(
            functools.partial(edge_kernel, band, cols),
            tiles,
            1000,
            [pltpu.VMEM((2 * HALO, 2 * local, width), BF16)],
        )(own, far, near)
        recv = lax.all_to_all(packed, "rot", 0, 0, tiled=True)
    with jax.named_scope("weights"):
        fwd = jnp.transpose(filters, (1, 2, 0, 3)).reshape(taps, CH, n)
        back = jnp.concatenate([filters[:1], filters[:0:-1]], axis=0)
        bwd = jnp.transpose(back, (1, 3, 0, 2)).reshape(taps, CH, n)
        bias2 = jnp.broadcast_to(bias[:, None], (CH, size))
        recv, fwd, bwd, bias2 = lax.optimization_barrier((recv, fwd, bwd, bias2))
    with jax.named_scope("grad"):
        half = shaped((groups, 9 * 8, 4 * CH), F32)
        g, keep, give = call(
            functools.partial(grad_kernel, band, cols),
            (shaped((n, size), BF16), half, half),
            2 * 18 * n * n * size,
            [pltpu.VMEM((4, size, 2 * n), BF16), square],
        )(recv, fwd, bias2)
    def met(i, along, pair):
        now = i // along % 4
        return i + (pair(now) - now) * along

    def add_four(v, pair, beside=None):
        v = v.astype(BF16)

        def swapped(to):
            return lax.ppermute(v, "rows", [(i, to(i)) for i in range(bands)])

        both = swapped(lambda i: met(met(i, 2, pair), 8, pair))
        deep = swapped(lambda i: met(i, 8, pair))
        wide = swapped(lambda i: met(i, 2, pair))
        if beside is not None:
            both, deep, wide, beside = lax.optimization_barrier((both, deep, wide, beside))
        v, both, deep, wide = [t.astype(F32) for t in (v, both, deep, wide)]
        return (v + both) + (deep + wide), beside

    with jax.named_scope("filter_core"):
        other = lax.ppermute(give, "rows", swap)
    with jax.named_scope("input_grad"):
        dx = call(
            functools.partial(input_kernel, band, cols),
            shaped((n, width), BF16),
            2 * 9 * n * n * size,
            [square],
        )(g, bwd)
    with jax.named_scope("to_channels"):
        terms = keep.shape[1]
        block = local + -(-terms // 16) * 16
        sent = call(join_kernel, shaped((groups, block, width), BF16), 1000)(
            keep, other, dx.reshape(groups, local, width)
        )
        got = lax.all_to_all(sent, "rot", 0, 0, tiled=True)
    with jax.named_scope("filter_rot"):
        v = jnp.sum(got[:, local : local + terms].astype(F32), axis=0)
    with jax.named_scope("input_grad"):
        input_grad = call(
            functools.partial(unpack_kernel, band, cols), shaped((n, width), BF16), 2 * n * n * width
        )(got[:, :local]).reshape(inputs.shape)
    with jax.named_scope("filter_blocks"):
        v, _ = add_four(v, lambda k: k ^ 1)
    with jax.named_scope("filter_rows"):
        v, input_grad = add_four(v, lambda k: 3 - k, input_grad)
    with jax.named_scope("filter_out"):
        scale = float(rotations * band * bands * width) ** (-0.5)
        other = lax.ppermute(v, "rows", swap)
        filter_grad = call(
            functools.partial(out_kernel, scale), shaped((2, taps, CH, CH), F32), 1000
        )(v, other)
    return input_grad, filter_grad


def solution(mesh):
    return jax.shard_map(
        shards,
        mesh=mesh,
        in_specs=(P("rot", "rows", None), P("rot", "rows", None), P(), P()),
        out_specs=(P("rot", "rows", None), P("rot", None, None, None)),
        check_vma=False,
    )
```

```python
import functools

import jax
import jax.numpy as jnp
from jax import lax
from jax.experimental import pallas as pl
from jax.experimental.pallas import tpu as pltpu
from jax.sharding import PartitionSpec as P

CH = 32
HALO = 2
GROUP = 16
F32 = jnp.float32
BF16 = jnp.bfloat16


def lanes(shape):
    return lax.broadcasted_iota(jnp.int32, shape, len(shape) - 1)


def spread(src, dst):
    n = src.shape[2]
    for a in range(3):
        for b in range(3):
            v = src[3 * a + b]
            for fine in range(4):
                t = v
                if fine:
                    cut = n - CH * fine
                    t = jnp.concatenate([v[:, cut:], v[:, :cut]], axis=1)
                for coarse in range(n // 128):
                    u = t
                    if coarse:
                        cut = n - 128 * coarse
                        u = jnp.concatenate([t[:, cut:], t[:, :cut]], axis=1)
                    row = b * n + CH * (4 * coarse + fine)
                    dst[row : row + CH, a * n : (a + 1) * n] = u


def exchanged(v, band, forth):
    n = v.shape[0]
    i = lax.broadcasted_iota(jnp.int32, (n, n), 0)
    j = lax.broadcasted_iota(jnp.int32, (n, n), 1)
    if forth:
        i, j = j, i
    one = (i // band == j % (n // band)) & (i % band == j // (n // band))
    return jnp.dot(one.astype(BF16), v, preferred_element_type=F32).astype(BF16)


def place_row(parts, v, r, j, cols):
    both, width = v.shape
    pitch = cols + 2 * HALO
    lane = lanes((both, width))
    low = pitch * r + max(HALO - cols * j, 0)
    high = pitch * r + min(pitch, width + HALO - cols * j)
    moved = pltpu.roll(v, (pitch * r - cols * j + HALO) % width, 1)
    for h in range(2):
        if low < width * (h + 1) and high > width * h:
            ok = (lane >= low - width * h) & (lane < high - width * h)
            parts[h] = jnp.where(ok, moved, parts[h])


def ends_kernel(band, x_ref, c_ref, far_ref, near_ref):
    n, width = x_ref.shape
    local = n // band
    upper = (lax.axis_index("rows") % 2) * (band - HALO)
    i = lax.broadcasted_iota(jnp.int32, (2 * HALO * local, n), 0)
    j = lax.broadcasted_iota(jnp.int32, (2 * HALO * local, n), 1)
    spot = i // local
    row = spot % HALO + jnp.where(spot < HALO, upper, band - HALO - upper)
    one = ((i % local == j // band) & (row == j % band)).astype(BF16)
    for part, ref in enumerate((x_ref, c_ref)):
        t = jnp.dot(one, ref[...], preferred_element_type=F32).astype(BF16)
        t = t.reshape(2 * HALO, local, width)
        far_ref[:, part * local : (part + 1) * local] = t[:HALO]
        near_ref[:, part * local : (part + 1) * local] = t[HALO:]


def own_kernel(band, cols, x_ref, c_ref, out_ref):
    groups, both, size = out_ref.shape
    width = size // 2
    turned = [
        exchanged(ref[...], band, True).reshape(band, both // 2, width) for ref in (x_ref, c_ref)
    ]
    rows = [jnp.concatenate([t[r] for t in turned], axis=0) for r in range(band)]
    for j in range(groups):
        parts = [jnp.zeros((both, width), BF16) for _ in range(2)]
        for r in range(band):
            place_row(parts, rows[r], r + HALO, j, cols)
        for h in range(2):
            out_ref[j, :, width * h : width * (h + 1)] = parts[h]


def edge_kernel(band, cols, own_ref, far_ref, near_ref, out_ref, edge_ref):
    groups, both, size = out_ref.shape
    width = size // 2
    upper = lax.axis_index("rows") % 2
    for c in range(2):

        @pl.when(upper == c)
        def _():
            edge_ref[:HALO] = (near_ref if c else far_ref)[...]
            edge_ref[HALO:] = (far_ref if c else near_ref)[...]

    for j in range(groups):
        parts = [own_ref[j, :, width * h : width * (h + 1)] for h in range(2)]
        for r in range(HALO):
            place_row(parts, edge_ref[r], r, j, cols)
            place_row(parts, edge_ref[HALO + r], r + HALO + band, j, cols)
        for h in range(2):
            out_ref[j, :, width * h : width * (h + 1)] = parts[h]


def inside(size, band, cols, ring):
    pitch = cols + 2 * HALO
    lane = lanes((1, size))
    row, col = lane // pitch, lane % pitch
    edge = HALO - ring
    return (row >= edge) & (row < band + 2 * HALO - edge) & (col >= edge) & (col < pitch - edge)


def lanes_turned(v, by):
    return jnp.concatenate([v[:, by:], v[:, :by]], axis=1) if by else v


def grad_kernel(band, cols, recv_ref, f_ref, bias_ref, g_ref, part_ref, xt_ref, w_ref):
    groups, both, size = recv_ref.shape
    half = both // 2
    n = groups * half
    rot = n // CH
    pitch = cols + 2 * HALO
    x = recv_ref[:, :half, :].reshape(n, size)
    cot = recv_ref[:, half:, :].reshape(n, size)
    spread(f_ref, w_ref)
    x3 = jnp.concatenate([pltpu.roll(x, pitch, 1), x, pltpu.roll(x, size - pitch, 1)], axis=0)
    parts = [
        jnp.dot(w_ref[b * n : (b + 1) * n, :], x3, preferred_element_type=F32) for b in range(3)
    ]
    bias = jnp.concatenate([bias_ref[...]] * rot, axis=0)
    pre = parts[1] + pltpu.roll(parts[0], 1, 1) + pltpu.roll(parts[2], size - 1, 1) + bias
    sigma = jax.nn.sigmoid(pre)
    grad = cot.astype(F32) * sigma * (1.0 + pre * (1.0 - sigma))
    grad = jnp.where(inside(size, band, cols, 1), grad, 0.0)
    g_ref[...] = grad.astype(BF16)
    own = jnp.where(inside(size, band, cols, 0), grad, 0.0).astype(BF16)
    moved = [
        pltpu.roll(own, (pitch * (a - 1) + b - 1) % size, 1) if (a, b) != (1, 1) else own
        for a in range(3)
        for b in range(3)
    ]
    turned = x.T
    for fine in range(4):
        v = lanes_turned(turned, CH * fine)
        xt_ref[fine, :, :n] = v
        xt_ref[fine, :, n:] = v
    total = None
    for first in range(0, rot, GROUP):
        turns = range(first, first + GROUP)
        g8 = [jnp.concatenate([t[CH * r : CH * (r + 1)] for t in moved[:8]], axis=0) for r in turns]
        xs = [xt_ref[r % 4, :, 128 * (r // 4) : 128 * (r // 4) + n] for r in turns]
        d = jnp.dot(
            jnp.concatenate(g8, axis=1), jnp.concatenate(xs, axis=0), preferred_element_type=F32
        )
        total = d if total is None else total + d
    d = jnp.dot(moved[8], turned, preferred_element_type=F32)
    last = jnp.zeros((CH, n), F32)
    for fine in range(4):
        lined = None
        for coarse in range(rot // 4):
            r = 4 * coarse + fine
            e = lanes_turned(d[CH * r : CH * (r + 1)], 128 * coarse)
            lined = e if lined is None else lined + e
        last = last + lanes_turned(lined, CH * fine)
    spots = lanes((2 * CH, 128)) // CH
    spots8 = lanes((8, 128)) // CH
    taken = []
    for s in range(rot):
        at = slice(128 * (s // 4), 128 * (s // 4 + 1))
        wide = [total[2 * CH * t : 2 * CH * (t + 1), at] for t in range(4)]
        thin = [last[8 * t : 8 * (t + 1), at] for t in range(4)]
        for pieces, where in ((wide, spots), (thin, spots8)):
            out = None
            for t in range(4):
                by = CH * ((t - s) % 4)
                v = pltpu.roll(pieces[t], by, 1) if by else pieces[t]
                out = v if out is None else jnp.where(where == t, v, out)
            taken.append(out)
    for at, v in enumerate(taken):
        start = at // 2 % 2 * 9 * 8 + at % 2 * 2 * CH
        part_ref[at // 4, start : start + v.shape[0]] = v


def input_kernel(band, cols, g_ref, f_ref, out_ref, w_ref):
    n, size = g_ref.shape
    pitch = cols + 2 * HALO
    spread(f_ref, w_ref)
    g = g_ref[...]
    g3 = jnp.concatenate([pltpu.roll(g, size - pitch, 1), g, pltpu.roll(g, pitch, 1)], axis=0)
    parts = [
        jnp.dot(w_ref[b * n : (b + 1) * n, :], g3, preferred_element_type=F32) for b in range(3)
    ]
    grad = parts[1] + pltpu.roll(parts[0], size - 1, 1) + pltpu.roll(parts[2], 1, 1)
    grad = grad.astype(BF16)
    width = out_ref.shape[1]
    lane = lanes((n, width))
    out = jnp.zeros((n, width), BF16)
    for r in range(band):
        at = pitch * (r + HALO) + HALO
        for h in range(size // width):
            low, high = max(at, width * h), min(at + cols, width * (h + 1))
            if low < high:
                piece = pltpu.roll(grad[:, width * h : width * (h + 1)], (cols * r - at) % width, 1)
                low, high = low - at + cols * r, high - at + cols * r
                out = jnp.where((lane >= low) & (lane < high), piece, out)
    out_ref[...] = out


def join_kernel(part_ref, other_ref, dx_ref, out_ref):
    groups, terms, width = part_ref.shape
    local = dx_ref.shape[1]
    out_ref[:, :local] = dx_ref[...]
    out_ref[:, local:] = (part_ref[...] + other_ref[...]).astype(BF16)


def unpack_kernel(band, cols, dx_ref, out_ref):
    groups, local, width = dx_ref.shape
    lane = lanes((local, width))
    rows = []
    for r in range(band):
        out = jnp.zeros((local, width), BF16)
        for j in range(groups):
            piece = pltpu.roll(dx_ref[j], (cols * (j - r)) % width, 1)
            out = jnp.where((lane >= cols * j) & (lane < cols * (j + 1)), piece, out)
        rows.append(out)
    out_ref[...] = exchanged(jnp.concatenate(rows, axis=0), band, False)


def out_kernel(scale, v_ref, out_ref):
    for part in range(2):
        v = v_ref[9 * 8 * part : 9 * 8 * (part + 1)] * scale
        for tap in range(8):
            row, at = CH * (tap % 2), CH * (tap // 2)
            out_ref[part, tap] = v[row : row + CH, at : at + CH]
        for t in range(4):
            out_ref[part, 8, 8 * t : 8 * (t + 1)] = v[2 * CH :, CH * t : CH * (t + 1)]


def shaped(shape, dtype):
    return jax.ShapeDtypeStruct(shape, dtype)


def call(kernel, outs, flops, scratch=(), limit=24, **specs):
    return pl.pallas_call(
        kernel,
        out_shape=outs,
        scratch_shapes=list(scratch),
        **specs,
        compiler_params=pltpu.CompilerParams(vmem_limit_bytes=limit * 1024 * 1024),
        cost_estimate=pl.CostEstimate(flops=flops, bytes_accessed=2_000_000, transcendentals=0),
    )


def shards(inputs, cotangent, filters, bias):
    local, band, width = inputs.shape
    rotations, taps = filters.shape[:2]
    n = rotations * CH
    groups = lax.axis_size("rot")
    bands = lax.axis_size("rows")
    cols = width // groups
    size = 2 * width
    across = [(i, j) for i in range(1, bands - 1, 2) for i, j in ((i, i + 1), (i + 1, i))]
    swap = [(i, i ^ 1) for i in range(bands)]
    square = pltpu.VMEM((3 * n, 3 * n), BF16)

    with jax.named_scope("edge_rows"):
        x, c = inputs.reshape(n, width), cotangent.reshape(n, width)
        edge = shaped((HALO, 2 * local, width), BF16)
        far, near = call(functools.partial(ends_kernel, band), (edge, edge), 1000)(x, c)
        far = lax.ppermute(far, "rows", across)
        near = lax.ppermute(near, "rows", swap)
    with jax.named_scope("to_tiles"):
        tiles = shaped((groups, 2 * local, size), BF16)
        own = call(functools.partial(own_kernel, band, cols), tiles, 4 * n * n * width)(
            x, c
        )
        packed = call(
            functools.partial(edge_kernel, band, cols),
            tiles,
            1000,
            [pltpu.VMEM((2 * HALO, 2 * local, width), BF16)],
        )(own, far, near)
        recv = lax.all_to_all(packed, "rot", 0, 0, tiled=True)
    with jax.named_scope("weights"):
        fwd = jnp.transpose(filters, (1, 2, 0, 3)).reshape(taps, CH, n)
        back = jnp.concatenate([filters[:1], filters[:0:-1]], axis=0)
        bwd = jnp.transpose(back, (1, 3, 0, 2)).reshape(taps, CH, n)
        bias2 = jnp.broadcast_to(bias[:, None], (CH, size))
        recv, fwd, bwd, bias2 = lax.optimization_barrier((recv, fwd, bwd, bias2))
    with jax.named_scope("grad"):
        g, part = call(
            functools.partial(grad_kernel, band, cols),
            (shaped((n, size), BF16), shaped((groups, 2 * 9 * 8, 4 * CH), F32)),
            2 * 18 * n * n * size,
            [pltpu.VMEM((4, size, 2 * n), BF16), square],
        )(recv, fwd, bias2)
    def met(i, along, pair):
        now = i // along % 4
        return i + (pair(now) - now) * along

    def add_four(v, pair, beside=None):
        v = v.astype(BF16)

        def swapped(to):
            return lax.ppermute(v, "rows", [(i, to(i)) for i in range(bands)])

        both = swapped(lambda i: met(met(i, 2, pair), 8, pair))
        deep = swapped(lambda i: met(i, 8, pair))
        wide = swapped(lambda i: met(i, 2, pair))
        if beside is not None:
            both, deep, wide, beside = lax.optimization_barrier((both, deep, wide, beside))
        v, both, deep, wide = [t.astype(F32) for t in (v, both, deep, wide)]
        return (v + both) + (deep + wide), beside

    with jax.named_scope("filter_core"):
        other = lax.ppermute(part, "rows", swap)
    with jax.named_scope("input_grad"):
        dx = call(
            functools.partial(input_kernel, band, cols),
            shaped((n, width), BF16),
            2 * 9 * n * n * size,
            [square],
        )(g, bwd)
    with jax.named_scope("to_channels"):
        terms = part.shape[1]
        block = local + terms
        sent = call(join_kernel, shaped((groups, block, width), BF16), 1000)(
            part, other, dx.reshape(groups, local, width)
        )
        got = lax.all_to_all(sent, "rot", 0, 0, tiled=True)
    with jax.named_scope("filter_rot"):
        v = jnp.sum(got[:, local : local + terms].astype(F32), axis=0)
    with jax.named_scope("input_grad"):
        input_grad = call(
            functools.partial(unpack_kernel, band, cols), shaped((n, width), BF16), 2 * n * n * width
        )(got[:, :local]).reshape(inputs.shape)
    with jax.named_scope("filter_blocks"):
        v, _ = add_four(v, lambda k: k ^ 1)
    with jax.named_scope("filter_rows"):
        v, input_grad = add_four(v, lambda k: 3 - k, input_grad)
    with jax.named_scope("filter_out"):
        scale = float(rotations * band * bands * width) ** (-0.5)
        filter_grad = call(
            functools.partial(out_kernel, scale), shaped((2, taps, CH, CH), F32), 1000
        )(v)
    return input_grad, filter_grad


def solution(mesh):
    return jax.shard_map(
        shards,
        mesh=mesh,
        in_specs=(P("rot", "rows", None), P("rot", "rows", None), P(), P()),
        out_specs=(P("rot", "rows", None), P("rot", None, None, None)),
        check_vma=False,
    )
```

```python
import functools

import jax
import jax.numpy as jnp
from jax import lax
from jax.experimental import pallas as pl
from jax.experimental.pallas import tpu as pltpu
from jax.sharding import PartitionSpec as P

CH = 32
HALO = 2
GROUP = 16
F32 = jnp.float32
BF16 = jnp.bfloat16


def lanes(shape):
    return lax.broadcasted_iota(jnp.int32, shape, len(shape) - 1)


def spread(src, dst):
    n = src.shape[2]
    for a in range(3):
        for b in range(3):
            v = src[3 * a + b]
            for fine in range(4):
                t = v
                if fine:
                    cut = n - CH * fine
                    t = jnp.concatenate([v[:, cut:], v[:, :cut]], axis=1)
                for coarse in range(n // 128):
                    u = t
                    if coarse:
                        cut = n - 128 * coarse
                        u = jnp.concatenate([t[:, cut:], t[:, :cut]], axis=1)
                    row = b * n + CH * (4 * coarse + fine)
                    dst[row : row + CH, a * n : (a + 1) * n] = u


def exchanged(v, band, forth):
    n = v.shape[0]
    i = lax.broadcasted_iota(jnp.int32, (n, n), 0)
    j = lax.broadcasted_iota(jnp.int32, (n, n), 1)
    if forth:
        i, j = j, i
    one = (i // band == j % (n // band)) & (i % band == j // (n // band))
    return jnp.dot(one.astype(BF16), v, preferred_element_type=F32).astype(BF16)


def place_row(parts, v, r, j, cols):
    both, width = v.shape
    pitch = cols + 2 * HALO
    lane = lanes((both, width))
    low = pitch * r + max(HALO - cols * j, 0)
    high = pitch * r + min(pitch, width + HALO - cols * j)
    moved = pltpu.roll(v, (pitch * r - cols * j + HALO) % width, 1)
    for h in range(2):
        if low < width * (h + 1) and high > width * h:
            ok = (lane >= low - width * h) & (lane < high - width * h)
            parts[h] = jnp.where(ok, moved, parts[h])


def ends_kernel(band, x_ref, c_ref, far_ref, near_ref):
    n, width = x_ref.shape
    local = n // band
    upper = (lax.axis_index("rows") % 2) * (band - HALO)
    i = lax.broadcasted_iota(jnp.int32, (2 * HALO * local, n), 0)
    j = lax.broadcasted_iota(jnp.int32, (2 * HALO * local, n), 1)
    spot = i // local
    row = spot % HALO + jnp.where(spot < HALO, upper, band - HALO - upper)
    one = ((i % local == j // band) & (row == j % band)).astype(BF16)
    for part, ref in enumerate((x_ref, c_ref)):
        t = jnp.dot(one, ref[...], preferred_element_type=F32).astype(BF16)
        t = t.reshape(2 * HALO, local, width)
        far_ref[:, part * local : (part + 1) * local] = t[:HALO]
        near_ref[:, part * local : (part + 1) * local] = t[HALO:]


def own_kernel(band, cols, x_ref, c_ref, out_ref):
    groups, both, size = out_ref.shape
    width = size // 2
    turned = [
        exchanged(ref[...], band, True).reshape(band, both // 2, width) for ref in (x_ref, c_ref)
    ]
    rows = [jnp.concatenate([t[r] for t in turned], axis=0) for r in range(band)]
    for j in range(groups):
        parts = [jnp.zeros((both, width), BF16) for _ in range(2)]
        for r in range(band):
            place_row(parts, rows[r], r + HALO, j, cols)
        for h in range(2):
            out_ref[j, :, width * h : width * (h + 1)] = parts[h]


def edge_kernel(band, cols, own_ref, far_ref, near_ref, out_ref, edge_ref):
    groups, both, size = out_ref.shape
    width = size // 2
    upper = lax.axis_index("rows") % 2
    for c in range(2):

        @pl.when(upper == c)
        def _():
            edge_ref[:HALO] = (near_ref if c else far_ref)[...]
            edge_ref[HALO:] = (far_ref if c else near_ref)[...]

    for j in range(groups):
        parts = [own_ref[j, :, width * h : width * (h + 1)] for h in range(2)]
        for r in range(HALO):
            place_row(parts, edge_ref[r], r, j, cols)
            place_row(parts, edge_ref[HALO + r], r + HALO + band, j, cols)
        for h in range(2):
            out_ref[j, :, width * h : width * (h + 1)] = parts[h]


def inside(size, band, cols, ring):
    pitch = cols + 2 * HALO
    lane = lanes((1, size))
    row, col = lane // pitch, lane % pitch
    edge = HALO - ring
    return (row >= edge) & (row < band + 2 * HALO - edge) & (col >= edge) & (col < pitch - edge)


def lanes_turned(v, by):
    return jnp.concatenate([v[:, by:], v[:, :by]], axis=1) if by else v


def grad_kernel(band, cols, recv_ref, f_ref, bias_ref, g_ref, part_ref, xt_ref, w_ref):
    groups, both, size = recv_ref.shape
    half = both // 2
    n = groups * half
    rot = n // CH
    pitch = cols + 2 * HALO
    x = recv_ref[:, :half, :].reshape(n, size)
    cot = recv_ref[:, half:, :].reshape(n, size)
    spread(f_ref, w_ref)
    x3 = jnp.concatenate([pltpu.roll(x, pitch, 1), x, pltpu.roll(x, size - pitch, 1)], axis=0)
    parts = [
        jnp.dot(w_ref[b * n : (b + 1) * n, :], x3, preferred_element_type=F32) for b in range(3)
    ]
    bias = jnp.concatenate([bias_ref[...]] * rot, axis=0)
    pre = parts[1] + pltpu.roll(parts[0], 1, 1) + pltpu.roll(parts[2], size - 1, 1) + bias
    sigma = jax.nn.sigmoid(pre)
    grad = cot.astype(F32) * sigma * (1.0 + pre * (1.0 - sigma))
    grad = jnp.where(inside(size, band, cols, 1), grad, 0.0)
    g_ref[...] = grad.astype(BF16)
    own = jnp.where(inside(size, band, cols, 0), grad, 0.0).astype(BF16)
    moved = [
        pltpu.roll(own, (pitch * (a - 1) + b - 1) % size, 1) if (a, b) != (1, 1) else own
        for a in range(3)
        for b in range(3)
    ]
    turned = x.T
    for fine in range(4):
        v = lanes_turned(turned, CH * fine)
        xt_ref[fine, :, :n] = v
        xt_ref[fine, :, n:] = v
    total = None
    for first in range(0, rot, GROUP):
        turns = range(first, first + GROUP)
        g8 = [jnp.concatenate([t[CH * r : CH * (r + 1)] for t in moved[:8]], axis=0) for r in turns]
        xs = [xt_ref[r % 4, :, 128 * (r // 4) : 128 * (r // 4) + n] for r in turns]
        d = jnp.dot(
            jnp.concatenate(g8, axis=1), jnp.concatenate(xs, axis=0), preferred_element_type=F32
        )
        total = d if total is None else total + d
    d = jnp.dot(moved[8], turned, preferred_element_type=F32)
    last = jnp.zeros((CH, n), F32)
    for fine in range(4):
        lined = None
        for coarse in range(rot // 4):
            r = 4 * coarse + fine
            e = lanes_turned(d[CH * r : CH * (r + 1)], 128 * coarse)
            lined = e if lined is None else lined + e
        last = last + lanes_turned(lined, CH * fine)
    spots = lanes((2 * CH, 128)) // CH
    spots8 = lanes((8, 128)) // CH
    taken = []
    for s in range(rot):
        at = slice(128 * (s // 4), 128 * (s // 4 + 1))
        wide = [total[2 * CH * t : 2 * CH * (t + 1), at] for t in range(4)]
        thin = [last[8 * t : 8 * (t + 1), at] for t in range(4)]
        for pieces, where in ((wide, spots), (thin, spots8)):
            out = None
            for t in range(4):
                by = CH * ((t - s) % 4)
                v = pltpu.roll(pieces[t], by, 1) if by else pieces[t]
                out = v if out is None else jnp.where(where == t, v, out)
            taken.append(out)
    for at, v in enumerate(taken):
        start = at // 2 % 2 * 9 * 8 + at % 2 * 2 * CH
        part_ref[at // 4, start : start + v.shape[0]] = v


def input_kernel(band, cols, g_ref, f_ref, out_ref, w_ref):
    n, size = g_ref.shape
    pitch = cols + 2 * HALO
    spread(f_ref, w_ref)
    g = g_ref[...]
    g3 = jnp.concatenate([pltpu.roll(g, size - pitch, 1), g, pltpu.roll(g, pitch, 1)], axis=0)
    parts = [
        jnp.dot(w_ref[b * n : (b + 1) * n, :], g3, preferred_element_type=F32) for b in range(3)
    ]
    grad = parts[1] + pltpu.roll(parts[0], size - 1, 1) + pltpu.roll(parts[2], 1, 1)
    grad = grad.astype(BF16)
    width = out_ref.shape[1]
    lane = lanes((n, width))
    out = jnp.zeros((n, width), BF16)
    for r in range(band):
        at = pitch * (r + HALO) + HALO
        for h in range(size // width):
            low, high = max(at, width * h), min(at + cols, width * (h + 1))
            if low < high:
                piece = pltpu.roll(grad[:, width * h : width * (h + 1)], (cols * r - at) % width, 1)
                low, high = low - at + cols * r, high - at + cols * r
                out = jnp.where((lane >= low) & (lane < high), piece, out)
    out_ref[...] = out


def join_kernel(part_ref, other_ref, dx_ref, out_ref):
    groups, terms, width = part_ref.shape
    local = dx_ref.shape[1]
    out_ref[:, :local] = dx_ref[...]
    out_ref[:, local:] = (part_ref[...] + other_ref[...]).astype(BF16)


def unpack_kernel(band, cols, dx_ref, out_ref):
    groups, local, width = dx_ref.shape
    lane = lanes((local, width))
    rows = []
    for r in range(band):
        out = jnp.zeros((local, width), BF16)
        for j in range(groups):
            piece = pltpu.roll(dx_ref[j], (cols * (j - r)) % width, 1)
            out = jnp.where((lane >= cols * j) & (lane < cols * (j + 1)), piece, out)
        rows.append(out)
    out_ref[...] = exchanged(jnp.concatenate(rows, axis=0), band, False)


def out_kernel(scale, v_ref, out_ref):
    for part in range(2):
        v = v_ref[9 * 8 * part : 9 * 8 * (part + 1)] * scale
        for tap in range(8):
            row, at = CH * (tap % 2), CH * (tap // 2)
            out_ref[part, tap] = v[row : row + CH, at : at + CH]
        for t in range(4):
            out_ref[part, 8, 8 * t : 8 * (t + 1)] = v[2 * CH :, CH * t : CH * (t + 1)]


def shaped(shape, dtype):
    return jax.ShapeDtypeStruct(shape, dtype)


def call(kernel, outs, flops, scratch=(), limit=24, **specs):
    return pl.pallas_call(
        kernel,
        out_shape=outs,
        scratch_shapes=list(scratch),
        **specs,
        compiler_params=pltpu.CompilerParams(vmem_limit_bytes=limit * 1024 * 1024),
        cost_estimate=pl.CostEstimate(flops=flops, bytes_accessed=2_000_000, transcendentals=0),
    )


def shards(inputs, cotangent, filters, bias):
    local, band, width = inputs.shape
    rotations, taps = filters.shape[:2]
    n = rotations * CH
    groups = lax.axis_size("rot")
    bands = lax.axis_size("rows")
    cols = width // groups
    size = 2 * width
    across = [(i, j) for i in range(1, bands - 1, 2) for i, j in ((i, i + 1), (i + 1, i))]
    swap = [(i, i ^ 1) for i in range(bands)]
    square = pltpu.VMEM((3 * n, 3 * n), BF16)

    with jax.named_scope("edge_rows"):
        x, c = inputs.reshape(n, width), cotangent.reshape(n, width)
        edge = shaped((HALO, 2 * local, width), BF16)
        far, near = call(functools.partial(ends_kernel, band), (edge, edge), 1000)(x, c)
        far = lax.ppermute(far, "rows", across)
        near = lax.ppermute(near, "rows", swap)
    with jax.named_scope("to_tiles"):
        tiles = shaped((groups, 2 * local, size), BF16)
        own = call(functools.partial(own_kernel, band, cols), tiles, 4 * n * n * width)(
            x, c
        )
        packed = call(
            functools.partial(edge_kernel, band, cols),
            tiles,
            1000,
            [pltpu.VMEM((2 * HALO, 2 * local, width), BF16)],
        )(own, far, near)
        recv = lax.all_to_all(packed, "rot", 0, 0, tiled=True)
    with jax.named_scope("weights"):
        fwd = jnp.transpose(filters, (1, 2, 0, 3)).reshape(taps, CH, n)
        back = jnp.concatenate([filters[:1], filters[:0:-1]], axis=0)
        bwd = jnp.transpose(back, (1, 3, 0, 2)).reshape(taps, CH, n)
        bias2 = jnp.broadcast_to(bias[:, None], (CH, size))
        recv, fwd, bwd, bias2 = lax.optimization_barrier((recv, fwd, bwd, bias2))
    with jax.named_scope("grad"):
        g, part = call(
            functools.partial(grad_kernel, band, cols),
            (shaped((n, size), BF16), shaped((groups, 2 * 9 * 8, 4 * CH), F32)),
            2 * 18 * n * n * size,
            [pltpu.VMEM((4, size, 2 * n), BF16), square],
        )(recv, fwd, bias2)
    def turn(i, step, by):
        now = i // step % 4
        return i + ((now + by) % 4 - now) * step

    def add_four(v, step, beside=None):
        v = v.astype(BF16)
        far, near, back = [
            lax.ppermute(v, "rows", [(i, turn(i, step, by)) for i in range(bands)]) for by in (2, 1, 3)
        ]
        if beside is not None:
            far, near, back, beside = lax.optimization_barrier((far, near, back, beside))
        v, far, near, back = [t.astype(F32) for t in (v, far, near, back)]
        return (v + far) + (near + back), beside

    with jax.named_scope("filter_core"):
        other = lax.ppermute(part, "rows", swap)
    with jax.named_scope("input_grad"):
        dx = call(
            functools.partial(input_kernel, band, cols),
            shaped((n, width), BF16),
            2 * 9 * n * n * size,
            [square],
        )(g, bwd)
    with jax.named_scope("to_channels"):
        terms = part.shape[1]
        block = local + terms
        sent = call(join_kernel, shaped((groups, block, width), BF16), 1000)(
            part, other, dx.reshape(groups, local, width)
        )
        got = lax.all_to_all(sent, "rot", 0, 0, tiled=True)
    with jax.named_scope("filter_rot"):
        v = jnp.sum(got[:, local : local + terms].astype(F32), axis=0)
    with jax.named_scope("input_grad"):
        input_grad = call(
            functools.partial(unpack_kernel, band, cols), shaped((n, width), BF16), 2 * n * n * width
        )(got[:, :local]).reshape(inputs.shape)
    with jax.named_scope("filter_y"):
        v, _ = add_four(v, 2)
    with jax.named_scope("filter_z"):
        v, input_grad = add_four(v, 8, input_grad)
    with jax.named_scope("filter_out"):
        scale = float(rotations * band * bands * width) ** (-0.5)
        filter_grad = call(
            functools.partial(out_kernel, scale), shaped((2, taps, CH, CH), F32), 1000
        )(v)
    return input_grad, filter_grad


def solution(mesh):
    return jax.shard_map(
        shards,
        mesh=mesh,
        in_specs=(P("rot", "rows", None), P("rot", "rows", None), P(), P()),
        out_specs=(P("rot", "rows", None), P("rot", None, None, None)),
        check_vma=False,
    )
```
